512 devices in a mesh: seq: 64 (over z, y), mp: 8 (over x, core).
Axes of the slice: x: 4, y: 4, z: 16, core: 2. Of those that a mesh axis runs over, the one named last changes fastest.
Arguments:
- tokens: bfloat16 [4, 4096, 1280], P(None, 'seq', 'mp')
- visible_lists: int32 [64, 64, 1], P('seq'), may hold values from 0 to 255, as said below
- visible_counts: int32 [64, 64], P('seq'), may hold values from 0 to 1, as said below
- w_in: bfloat16 [1280, 5120], P(None, 'mp'), may hold values from -0.15625 to 0.15625
- w_out: bfloat16 [5120, 1280], P('mp'), may hold values from -0.078125 to 0.078125
- w_embed: bfloat16 [1280, 512], P('mp'), may hold values from -0.15625 to 0.15625
- mask_token: bfloat16 [512], replicated, may hold values from -5 to 5
- positions: bfloat16 [4096, 512], P('seq'), may hold values from -5 to 5
- w_qkv: bfloat16 [512, 3, 512], P(None, None, 'mp')
- w_attn_out: bfloat16 [512, 512], P('mp'), may hold values from -0.25 to 0.25
Outputs:
- decoded: bfloat16 [4, 4096, 512], P(None, 'seq', 'mp')
The draws below stay inside these ranges and needn't reach their ends.
Inputs may be any that keep to these rules, and one draw needn't show every extreme that they name: `visible_lists`: every entry is a row of the sending block, 0 to 255; the 64 entries of one block are all different. `visible_counts`: one block fills every slot to every peer; the live slots of a block toward the peers differ by at most one in number.
All inputs are finite; a program needn't handle non-finite values.
Results may differ from the reference program's by a relative error of at most 0.024.
The reference program's roundings to bfloat16 on the way count: a program that leaves them out, or rounds other values in their place, can miss the bound.
Values may be sent and summed in bfloat16 or wider, within the bound.
No kernel may reach another device: no remote copies, remote signals or barrier semaphores. Data moves between devices by JAX's collectives and lax.ppermute only.
A program may use at most 64 MiB of HBM per device.

```python
import math
import jax
import jax.numpy as jnp
from jax import lax

D = 1280
FF = 5120
DD = 512
DHEADS = 16
HDIM = 32
TUB_DEV = 64
VOLS = 4
TUBELETS = 4096
VIS_DEV = 64
CAP = 1
N_SEQ = 64


def visible_plan(key):
    key_level, key_top, key_perm = jax.random.split(key, 3)
    rows_dev = VOLS * TUB_DEV
    levels = jax.random.randint(key_level, (N_SEQ,), 0, 4)
    busiest = jax.random.randint(key_top, (), 0, N_SEQ)
    levels = jnp.where(jnp.arange(N_SEQ) == busiest, 0, levels)
    live_count = VIS_DEV // jnp.left_shift(jnp.ones((N_SEQ,), jnp.int32), levels)
    orders = jax.vmap(jax.random.permutation, in_axes=(0, None))(jax.random.split(key_perm, N_SEQ), rows_dev)
    source = jnp.arange(N_SEQ, dtype=jnp.int32)[:, None, None]
    target = jnp.arange(N_SEQ, dtype=jnp.int32)[None, :, None]
    slot_ids = jnp.arange(CAP, dtype=jnp.int32)[None, None, :]
    rank_ids = slot_ids * N_SEQ + (target - source) % N_SEQ
    row_lists = jnp.take_along_axis(orders.astype(jnp.int32), rank_ids.reshape(N_SEQ, N_SEQ * CAP), axis=1)
    row_lists = row_lists.reshape(N_SEQ, N_SEQ, CAP)
    used_slots = jnp.sum((rank_ids < live_count[:, None, None]).astype(jnp.int32), axis=2)
    return (row_lists.astype(jnp.int32), used_slots.astype(jnp.int32))


def draw_visible_lists(key, part):
    plan = visible_plan(key)
    return plan[0]


def draw_visible_counts(key, part):
    plan = visible_plan(key)
    return plan[1]


def draw_tokens(key, part):
    key = jax.random.fold_in(key, 11)
    key_base, key_row, key_col = jax.random.split(key, 3)
    shape = (VOLS, TUBELETS, D)
    row_scale = jnp.exp(jax.random.uniform(key_row, (VOLS, TUBELETS, 1), jnp.float32, math.log(0.3), math.log(3.0)))
    col_scale = jnp.exp(jax.random.uniform(key_col, (D,), jnp.float32, math.log(0.3), math.log(3.0)))
    base_draw = jax.random.normal(key_base, shape, jnp.float32)
    return (base_draw * row_scale * col_scale).astype(jnp.bfloat16)


def draw_w_qkv(key, part):
    key = jax.random.fold_in(key, 23)
    base_draw = jax.random.normal(key, (DD, 3, DD), jnp.float32) * DD ** (-0.5)
    return base_draw.astype(jnp.bfloat16)


def block_scale(key, extent, pieces, low, largest):
    loudness, own = 1.0, jax.random.fold_in(key, 6)
    for axis_at, parts in pieces:
        draws = jnp.exp(jax.random.uniform(jax.random.fold_in(own, axis_at), (parts,), jnp.float32, low / len(pieces), largest / len(pieces)))
        loudness = loudness * jnp.repeat(draws, extent[axis_at] // parts).reshape([-1 if axis == axis_at else 1 for axis in range(len(extent))])
    return loudness


def scatter_about(own_key, dims, scale, bound, shards=(), kind=jnp.bfloat16):
    result = scale * jax.random.normal(own_key, dims, jnp.float32)
    if shards:
        result = result * block_scale(own_key, dims, shards, -0.22, 0.18)
    return jnp.clip(result, -bound, bound).astype(kind)


def setup_inputs(seed: int = 0) -> dict:
    keys = jax.random.split(jax.random.key(seed), 11)
    tokens = draw_tokens(jax.random.fold_in(keys[10], 71), 0)
    visible_lists = draw_visible_lists(jax.random.fold_in(keys[10], 71), 0)
    visible_counts = draw_visible_counts(jax.random.fold_in(keys[10], 71), 0)
    w_in = scatter_about(keys[3], (D, FF), D ** -0.5, 0.15625, ((1, 8),))
    w_out = scatter_about(keys[4], (FF, D), FF ** -0.5, 0.078125, ((0, 8),))
    w_embed = scatter_about(keys[5], (D, DD), D ** -0.5, 0.15625, ((0, 8),))
    mask_token = scatter_about(keys[6], (DD,), 1.0, 5.0)
    positions = scatter_about(keys[7], (TUBELETS, DD), 1.0, 5.0, ((0, 64),))
    w_qkv = draw_w_qkv(jax.random.fold_in(keys[10], 71), 0)
    w_attn_out = scatter_about(keys[9], (DD, DD), DD ** -0.5, 0.25, ((0, 8),))
    return {"tokens": tokens, "visible_lists": visible_lists, "visible_counts": visible_counts, "w_in": w_in, "w_out": w_out, "w_embed": w_embed, "mask_token": mask_token, "positions": positions, "w_qkv": w_qkv, "w_attn_out": w_attn_out}


def layer_norm(values):
    mean_row = lax.optimization_barrier(jnp.mean(values, axis=-1, keepdims=True))
    spread = lax.optimization_barrier(jnp.mean((values - mean_row) * (values - mean_row), axis=-1, keepdims=True))
    return (values - mean_row) * lax.rsqrt(spread + 1e-05)

def reference(tokens, visible_lists, visible_counts, w_in, w_out, w_embed, mask_token, positions, w_qkv, w_attn_out):
    rows_dev = VOLS * TUB_DEV
    local_rows = tokens.reshape(VOLS, N_SEQ, TUB_DEV, D).transpose(1, 0, 2, 3).reshape(N_SEQ, rows_dev, D)
    slot_index = visible_lists.reshape(N_SEQ, VIS_DEV).astype(jnp.int32)
    slot_ids = jnp.arange(CAP, dtype=jnp.int32)
    live_slots = (slot_ids[None, None, :] < visible_counts[:, :, None]).reshape(N_SEQ, VIS_DEV)
    slot_rows = jnp.take_along_axis(local_rows, slot_index[:, :, None], axis=1).reshape(N_SEQ * VIS_DEV, D)
    normed = layer_norm(slot_rows.astype(jnp.float32)).astype(jnp.bfloat16)
    hidden_act = jax.nn.gelu(jnp.dot(normed, w_in, preferred_element_type=jnp.float32), approximate=False).astype(jnp.bfloat16)
    encoded = (slot_rows.astype(jnp.float32) + jnp.dot(hidden_act, w_out, preferred_element_type=jnp.float32)).astype(jnp.bfloat16)
    embedded = jnp.dot(encoded, w_embed, preferred_element_type=jnp.float32).astype(jnp.bfloat16).reshape(N_SEQ, VIS_DEV, DD)
    placed = jnp.where(live_slots[:, :, None], embedded.astype(jnp.float32), jnp.float32(0.0))
    device_ids = jnp.broadcast_to(jnp.arange(N_SEQ, dtype=jnp.int32)[:, None], (N_SEQ, VIS_DEV))
    gathered = jnp.zeros((N_SEQ, rows_dev, DD), jnp.float32).at[device_ids, slot_index].add(placed)
    seen_rows = jnp.zeros((N_SEQ, rows_dev), jnp.float32).at[device_ids, slot_index].add(live_slots.astype(jnp.float32))
    pos_rows = jnp.broadcast_to(positions.reshape(N_SEQ, 1, TUB_DEV, DD), (N_SEQ, VOLS, TUB_DEV, DD)).reshape(N_SEQ, rows_dev, DD)
    chosen = jnp.where(seen_rows[:, :, None] > 0, gathered, mask_token.astype(jnp.float32)[None, None, :])
    decoder_in = (chosen + pos_rows.astype(jnp.float32)).astype(jnp.bfloat16)
    decoder_in = decoder_in.reshape(N_SEQ, VOLS, TUB_DEV, DD).transpose(1, 0, 2, 3).reshape(VOLS * TUBELETS, DD)
    dec_normed = layer_norm(decoder_in.astype(jnp.float32)).astype(jnp.bfloat16)
    projected = jnp.dot(dec_normed, w_qkv.reshape(DD, 3 * DD), preferred_element_type=jnp.float32).astype(jnp.bfloat16)
    projected = projected.reshape(VOLS, TUBELETS, 3, DHEADS, HDIM)

    def split_heads(which):
        return projected[:, :, which].transpose(0, 2, 1, 3).reshape(VOLS * DHEADS, TUBELETS, HDIM)
    score_scale = 1.0 / math.sqrt(HDIM)

    def per_head(inputs):
        query_block, key_block, val_block = inputs
        scores = jnp.dot(query_block, key_block.T, preferred_element_type=jnp.float32) * score_scale
        top_score = lax.optimization_barrier(jnp.max(scores, axis=-1, keepdims=True))
        weights = jnp.exp(scores - top_score)
        totals = lax.optimization_barrier(jnp.sum(weights, axis=-1, keepdims=True))
        return jnp.dot(weights.astype(jnp.bfloat16), val_block, preferred_element_type=jnp.float32) / totals
    attended = lax.map(per_head, (split_heads(0), split_heads(1), split_heads(2)))
    attended = attended.reshape(VOLS, DHEADS, TUBELETS, HDIM).transpose(0, 2, 1, 3).reshape(VOLS * TUBELETS, DD).astype(jnp.bfloat16)
    decoded = decoder_in.astype(jnp.float32) + jnp.dot(attended, w_attn_out, preferred_element_type=jnp.float32)
    return decoded.astype(jnp.bfloat16).reshape(VOLS, TUBELETS, DD)
```

```python
import math

import jax
import jax.numpy as jnp
from jax import lax
from jax.sharding import Mesh, PartitionSpec as P

HDIM = 32
MP = ("x", "core")
BF = jnp.bfloat16
F32 = jnp.float32


def layer_norm(values):
    mean_row = jnp.mean(values, axis=-1, keepdims=True)
    spread = jnp.mean((values - mean_row) * (values - mean_row), axis=-1, keepdims=True)
    return (values - mean_row) * lax.rsqrt(spread + 1e-05)


def dot(a, b):
    return jnp.dot(a, b, preferred_element_type=F32)


def spread_out(part, axes):
    count = lax.axis_size(axes)
    return lax.all_to_all(
        jnp.broadcast_to(part[None], (count, *part.shape)), axes, 0, 0, tiled=True
    )


def pieces(values, count):
    out = []
    for _ in range(count):
        top = lax.reduce_precision(values, 8, 7)
        out.append(top.astype(BF))
        values = values - top
    return out


def place(picked, slot_vals, other_vals):
    seen = jnp.sum(picked.astype(F32), axis=-1, keepdims=True) > 0
    return jnp.where(seen, dot(picked, slot_vals).astype(BF), other_vals)


def local(
    tokens,
    visible_lists,
    visible_counts,
    w_in,
    w_out,
    w_embed,
    mask_token,
    positions,
    w_qkv,
    w_attn_out,
):
    vols, tubs, part = tokens.shape
    rows = vols * tubs
    mp_index = lax.axis_index(MP)
    mp_count = lax.axis_size(MP)
    nz = lax.axis_size("z")
    ny = lax.axis_size("y")
    dec = w_embed.shape[1]
    dec_part = dec // mp_count
    flat = tokens.reshape(rows, part)
    ids = visible_lists.reshape(-1)
    slots = ids.shape[0]
    live = visible_counts.reshape(-1) > 0
    live_ids = jnp.where(live, ids, rows)

    id_rows = jnp.zeros((16, dec), BF).at[0, :slots].set(live_ids.astype(BF))
    packed = jnp.concatenate([positions, id_rows], axis=0)
    column = lax.all_gather(packed, "z")

    named = (ids[:, None] == jnp.arange(rows, dtype=jnp.int32)[None, :]).astype(BF)
    own = dot(named, flat).astype(BF)
    full = spread_out(own, MP).transpose(1, 0, 2).reshape(slots, mp_count * part)
    normed = layer_norm(full.astype(F32)).astype(BF)
    hidden = jax.nn.gelu(dot(normed, w_in), approximate=False).astype(BF)
    terms = dot(hidden, w_out).astype(BF)
    terms = terms.reshape(slots, mp_count, part).transpose(1, 0, 2)
    terms = lax.all_to_all(terms, MP, 0, 0, tiled=True)
    encoded = (own.astype(F32) + jnp.sum(terms.astype(F32), axis=0)).astype(BF)
    embed_terms = dot(encoded, w_embed).astype(BF)
    embedded = jnp.sum(spread_out(embed_terms, MP).astype(F32), axis=0).astype(BF)

    pos_pick = ((ids % tubs)[:, None] == jnp.arange(tubs, dtype=jnp.int32)[None, :]).astype(BF)
    slot_pos = dot(pos_pick, positions)
    slot_in = (embedded.astype(F32) + slot_pos).astype(BF)
    mask_in = (mask_token.astype(F32)[None, :] + positions.astype(F32)).astype(BF)
    head_width = w_qkv.shape[2]
    heads = head_width // HDIM
    w_flat = w_qkv.reshape(dec, 3 * head_width)
    both = jnp.concatenate([mask_in, slot_in], axis=0)
    projected = dot(layer_norm(both.astype(F32)).astype(BF), w_flat).astype(BF)
    mask_q = projected[:tubs, :head_width]
    slot_q = projected[tubs:, :head_width]
    slot_kv = projected[tubs:, head_width:]

    picked = (live_ids[None, :] == jnp.arange(rows, dtype=jnp.int32)[:, None]).astype(BF)
    queries = place(picked, slot_q, jnp.tile(mask_q, (vols, 1)))
    start = mp_index * dec_part
    dec_own = place(
        picked,
        lax.dynamic_slice_in_dim(slot_in, start, dec_part, 1),
        jnp.tile(lax.dynamic_slice_in_dim(mask_in, start, dec_part, 1), (vols, 1)),
    )

    plane_q = spread_out(queries, "y")
    column_slots = spread_out(slot_kv, "z")

    column_pos = column[:, :tubs].reshape(nz * tubs, dec)
    column_ids = column[:, tubs, :slots].astype(jnp.int32)
    column_mask = (mask_token.astype(F32)[None, :] + column_pos.astype(F32)).astype(BF)
    mask_kv = dot(layer_norm(column_mask.astype(F32)).astype(BF), w_flat[:, head_width:]).astype(BF)
    mask_kv = mask_kv.reshape(nz, tubs, 2 * head_width)
    column_picked = (
        column_ids[:, None, :] == jnp.arange(rows, dtype=jnp.int32)[None, :, None]
    ).astype(BF)
    placed = jnp.einsum("zrs,zsc->zrc", column_picked, column_slots, preferred_element_type=F32)
    seen = jnp.sum(column_picked.astype(F32), axis=-1, keepdims=True) > 0
    kv = jnp.where(seen, placed.astype(BF), jnp.tile(mask_kv, (1, vols, 1)))
    kv = kv.reshape(nz, vols, tubs, 2, heads, HDIM)
    keys = kv[:, :, :, 0].transpose(1, 3, 0, 2, 4).reshape(vols, heads, nz * tubs, HDIM)
    vals = kv[:, :, :, 1].transpose(1, 3, 0, 2, 4).reshape(vols, heads, nz * tubs, HDIM)
    qs = plane_q.reshape(ny, vols, tubs, heads, HDIM).transpose(1, 3, 0, 2, 4)
    qs = qs.reshape(vols, heads, ny * tubs, HDIM)
    scores = jnp.einsum("vhqd,vhkd->vhqk", qs, keys, preferred_element_type=F32)
    scores = scores * (1.0 / math.sqrt(HDIM))
    top = jnp.max(scores, axis=-1)
    weights = jnp.exp(scores - top[..., None])
    totals = jnp.sum(weights, axis=-1)
    summed = jnp.einsum("vhqk,vhkd->vhqd", weights.astype(BF), vals, preferred_element_type=F32)

    stats = jnp.stack([*pieces(top, 3), *pieces(totals, 2)], axis=-1)
    message = jnp.concatenate([summed.astype(BF), stats], axis=-1)
    width = HDIM + 5
    message = message.reshape(vols, heads, ny, tubs, width).transpose(2, 0, 3, 1, 4)
    message = message.reshape(ny, rows, heads * width)
    message = lax.all_to_all(message, "y", 0, 0, tiled=True)
    message = message.reshape(ny, rows, heads, width).astype(F32)
    tops = message[..., HDIM] + message[..., HDIM + 1] + message[..., HDIM + 2]
    fade = jnp.exp(tops - jnp.max(tops, axis=0, keepdims=True))
    total = jnp.sum(fade * (message[..., HDIM + 3] + message[..., HDIM + 4]), axis=0)
    attended = jnp.sum(fade[..., None] * message[..., :HDIM], axis=0) / total[..., None]
    attended = attended.reshape(rows, head_width).astype(BF)

    head_terms = dot(attended, w_attn_out).astype(BF)
    head_terms = head_terms.reshape(rows, mp_count, dec_part).transpose(1, 0, 2)
    head_terms = lax.all_to_all(head_terms, MP, 0, 0, tiled=True)
    decoded = dec_own.astype(F32) + jnp.sum(head_terms.astype(F32), axis=0)
    return decoded.astype(BF).reshape(vols, tubs, dec_part)


def solution(mesh):
    fine = Mesh(mesh.devices.reshape(16, 4, 4, 2), ("z", "y", "x", "core"))
    seq = ("z", "y")
    in_specs = (
        P(None, seq, MP),
        P(seq, None, None),
        P(seq, None),
        P(None, MP),
        P(MP, None),
        P(MP, None),
        P(),
        P(seq, None),
        P(None, None, MP),
        P(MP, None),
    )
    out_specs = P(None, seq, MP)
    return jax.shard_map(local, mesh=fine, in_specs=in_specs, out_specs=out_specs, check_vma=False)
```

```python
import functools
import math

import jax
import jax.numpy as jnp
from jax import lax
from jax.experimental import pallas as pl
from jax.experimental.pallas import tpu as pltpu
from jax.sharding import Mesh, PartitionSpec as P

HDIM = 32
MP = ("x", "core")
GROUP = ("zp", "y")
COLUMN = ("zz", "zp")
BF = jnp.bfloat16
F32 = jnp.float32
I32 = jnp.int32


def iota(shape, dim):
    return lax.broadcasted_iota(I32, shape, dim)


def dot(a, b):
    return jnp.dot(a, b, preferred_element_type=F32)


def dot_tn(a, b):
    return lax.dot_general(a, b, (((0,), (0,)), ((), ())), preferred_element_type=F32)


def dot_nt(a, b):
    return lax.dot_general(a, b, (((1,), (1,)), ((), ())), preferred_element_type=F32)


def norm_rows(values):
    mean_row = jnp.mean(values, axis=-1, keepdims=True)
    off = values - mean_row
    spread = jnp.mean(off * off, axis=-1, keepdims=True)
    return off * lax.rsqrt(spread + 1e-05)


def column_of(row):
    n = row.shape[1]
    return jnp.sum(jnp.where(iota((n, n), 0) == iota((n, n), 1), row, 0), axis=1, keepdims=True)


def live_row(lists, counts, rows):
    return jnp.where(counts > 0, lists, rows)


def fold_tail(block):
    tail = block[:, 128:]
    rows = tail.shape[0] // 4
    extra = jnp.concatenate([tail[k * rows : (k + 1) * rows] for k in range(4)], axis=1)
    return jnp.concatenate([block[:, :128], extra], axis=0)


def unfold_tail(folded):
    extra = folded[64:]
    tail = jnp.concatenate([extra[:, 32 * k : 32 * k + 32] for k in range(4)], axis=0)
    return jnp.concatenate([folded[:64], tail], axis=1)


def pick_kernel(lists, counts, tokens, out):
    rows = tokens.shape[0]
    ids = column_of(lists[...])
    named = (ids == iota((ids.shape[0], rows), 1)).astype(F32).astype(BF)
    own = fold_tail(dot(named, tokens[...])).astype(BF)
    for k in range(out.shape[0]):
        out[k] = own


def feed_kernel(gathered, w_in, w_out, out):
    count = gathered.shape[0]
    part = w_in.shape[0] // count
    blocks = [unfold_tail(gathered[k].astype(F32)) for k in range(count)]
    width = count * part
    mean_row = sum(jnp.sum(b, axis=1, keepdims=True) for b in blocks) * (1.0 / width)
    blocks = [b - mean_row for b in blocks]
    spread = sum(jnp.sum(b * b, axis=1, keepdims=True) for b in blocks) * (1.0 / width)
    scale = lax.rsqrt(spread + 1e-05)
    hidden = None
    for k in range(count):
        term = dot((blocks[k] * scale).astype(BF), w_in[k * part : (k + 1) * part, :])
        hidden = term if hidden is None else hidden + term
    act = (0.5 * hidden * (1.0 + lax.erf(hidden * math.sqrt(0.5)))).astype(BF)
    terms = dot(act, w_out[...])
    for k in range(count):
        out[k] = fold_tail(terms[:, k * part : (k + 1) * part]).astype(BF)


def embed_kernel(terms, own, w_embed, out):
    total = own[0].astype(F32) + sum(terms[k].astype(F32) for k in range(terms.shape[0]))
    encoded = unfold_tail(total).astype(BF)
    value = dot(encoded, w_embed[...]).astype(BF)
    for k in range(out.shape[0]):
        out[k] = value


def masked_kernel(mask_token, positions, w_all, out):
    mask_in = (mask_token[...].astype(F32) + positions[...].astype(F32)).astype(BF)
    out[...] = dot(norm_rows(mask_in.astype(F32)).astype(BF), w_all[...]).astype(BF)


def project_kernel(parts, lists, counts, positions, masked, w_all, slot_in, q_out, kv_out):
    tubs = positions.shape[0]
    slots = lists.shape[1]
    ids_row = live_row(lists[...], counts[...], 4 * tubs)
    ids = column_of(ids_row)
    embedded = sum(parts[k].astype(F32) for k in range(parts.shape[0])).astype(BF).astype(F32)
    at = (ids % tubs == iota((slots, tubs), 1)).astype(F32).astype(BF)
    row_in = (embedded + dot(at, positions[...])).astype(BF)
    slot_in[...] = row_in
    proj = dot(norm_rows(row_in.astype(F32)).astype(BF), w_all[...]).astype(BF)

    spot = (ids_row % tubs == iota((tubs, slots), 0)).astype(F32).astype(BF)
    of_volume = ids // tubs == iota((slots, 128), 1) // HDIM
    seen = dot(spot, of_volume.astype(F32).astype(BF)) > 0
    zero = jnp.zeros((slots, 128), BF)
    extra = jnp.concatenate(
        [
            jnp.concatenate([ids_row.astype(F32), jnp.zeros((1, 128 - slots), F32)], axis=1),
            jnp.zeros((15, 128), F32),
        ],
        axis=0,
    ).astype(BF)
    for head in range(2):
        cols = slice(128 * head, 128 * head + 128)
        placed = dot(spot, jnp.where(of_volume, proj[:, cols], zero))
        query = jnp.where(seen, placed, masked[:, cols].astype(F32)).astype(BF)
        for k in range(4):
            q_out[4 * head + k] = query
        cols = slice(256 + 64 * head, 256 + 64 * head + 64)
        block = jnp.concatenate([masked[:, cols], proj[:, cols]], axis=1)
        block = jnp.concatenate([block, extra], axis=0)
        for k in range(8):
            kv_out[2 * k + head] = block


def own_kernel(start, lists, counts, mask_token, positions, slot_in, out):
    tubs = positions.shape[0]
    feats, rows = out.shape
    slots = lists.shape[1]
    dec = positions.shape[1]
    ids = column_of(live_row(lists[...], counts[...], rows))
    choose = (iota((dec, feats), 0) == iota((dec, feats), 1) + start[0]).astype(F32).astype(BF)
    mask_in = (mask_token[...].astype(F32) + positions[...].astype(F32)).astype(BF)
    mask_own = dot(mask_in, choose).astype(BF)
    slot_own = dot(slot_in[...], choose).astype(BF)
    picked = (ids == iota((slots, rows), 1)).astype(F32)
    seen = jnp.sum(picked, axis=0, keepdims=True) > 0
    tile = (iota((tubs, rows), 0) == iota((tubs, rows), 1) % tubs).astype(F32).astype(BF)
    out[...] = jnp.where(seen, dot_tn(slot_own, picked.astype(BF)), dot_tn(mask_own, tile)).astype(BF)


def split_pieces(values, count):
    out = []
    for _ in range(count):
        top = values.astype(BF).astype(F32)
        out.append(top)
        values = values - top
    return out


def attend_kernel(queries, column, out, kv_scr, msg_scr):
    blocks, tubs = queries.shape[0], queries.shape[1]
    nz = column.shape[0]
    vols = 4
    rows = vols * tubs
    slots = 64
    keys = nz * tubs
    for k in range(nz):
        block = column[k, :tubs, :]
        ids_row = column[k, tubs : tubs + 16, :][0:1, :slots].astype(F32)
        picked = (ids_row == iota((rows, slots), 0).astype(F32)).astype(F32)
        seen = jnp.sum(picked, axis=1, keepdims=True) > 0
        placed = dot(picked.astype(BF), block[:, 64:])
        other = block[:, :64].astype(F32)
        other = jnp.concatenate([other] * vols, axis=0)
        mat = jnp.where(seen, placed, other).astype(BF)
        for v in range(vols):
            kv_scr[v, k * tubs : (k + 1) * tubs, :] = mat[v * tubs : (v + 1) * tubs]
    packed = queries[...].reshape(blocks * tubs, 128)
    scale = math.log2(math.e) / math.sqrt(HDIM)
    chunk = 256
    per = chunk // tubs
    for v in range(vols):
        lanes = iota((128, 64), 0)
        take = (lanes == iota((128, 64), 1) + HDIM * v) & (iota((128, 64), 1) < HDIM)
        query = dot(packed, take.astype(F32).astype(BF)).astype(BF)
        kv = kv_scr[v]
        for c in range(blocks // per):
            scores = dot_nt(kv, query[c * chunk : (c + 1) * chunk])
            top = jnp.max(scores, axis=0, keepdims=True)
            weights = jnp.exp2((scores - top) * scale)
            total = jnp.sum(weights, axis=0, keepdims=True)
            summed = dot_tn(kv, weights.astype(BF))[HDIM:]
            stats = jnp.concatenate(
                split_pieces(top * scale, 3) + split_pieces(total, 2) + [jnp.zeros((3, chunk), F32)],
                axis=0,
            )
            side = slice(64 * (v % 2), 64 * (v % 2) + 64)
            for b in range(per):
                cols = slice(b * tubs, (b + 1) * tubs)
                dest = c * per + b
                msg_scr[dest, HDIM * (v // 2) : HDIM * (v // 2) + HDIM, side] = summed[:, cols]
                msg_scr[dest, 64 + 8 * (v // 2) : 72 + 8 * (v // 2), side] = stats[:, cols]
    for b in range(blocks):
        out[b] = msg_scr[b].astype(BF)


def combine_kernel(message, w_attn_out, out):
    ny = 4
    parts = []
    for head in range(2):
        sides = []
        for u in range(2):
            stats = [message[4 * head + k, 64:, :].astype(F32)[8 * u : 8 * u + 8] for k in range(ny)]
            tops = [s[0:1] + s[1:2] + s[2:3] for s in stats]
            best = functools.reduce(jnp.maximum, tops)
            fades = [jnp.exp2(t - best) for t in tops]
            total = sum(f * (s[3:4] + s[4:5]) for f, s in zip(fades, stats))
            value = sum(
                f * message[4 * head + k, HDIM * u : HDIM * u + HDIM, :].astype(F32)
                for k, f in enumerate(fades)
            )
            sides.append(value / total)
        parts.append(jnp.concatenate(sides, axis=1))
    attended = jnp.concatenate(parts, axis=0).astype(BF)
    terms = dot_tn(w_attn_out[...], attended).astype(BF)
    count, feats, rows = out.shape
    for k in range(count):
        out[k] = terms[k * feats : (k + 1) * feats]


def finish_kernel(terms, dec_own, out):
    total = dec_own[...].astype(F32) + sum(terms[k].astype(F32) for k in range(terms.shape[0]))
    vols, tubs, feats = out.shape
    out[...] = total.T.astype(BF).reshape(vols, tubs, feats)


def call(kernel, out, *args, scratch=(), smem=0, cost=None):
    specs = [pl.BlockSpec(memory_space=pltpu.SMEM)] * smem
    specs += [pl.BlockSpec(memory_space=pltpu.VMEM)] * (len(args) - smem)
    many = isinstance(out, list)
    one = pl.BlockSpec(memory_space=pltpu.VMEM)
    return pl.pallas_call(
        kernel,
        out_shape=out,
        in_specs=specs,
        out_specs=[one] * len(out) if many else one,
        scratch_shapes=list(scratch),
        compiler_params=pltpu.CompilerParams(vmem_limit_bytes=32 * 2**20),
        cost_estimate=cost,
    )(*args)


def shape(*dims, dtype=BF):
    return jax.ShapeDtypeStruct(dims, dtype)


def exchange(values, axes):
    return lax.all_to_all(values, axes, 0, 0, tiled=True)


def local(
    tokens,
    visible_lists,
    visible_counts,
    w_in,
    w_out,
    w_embed,
    mask_token,
    positions,
    w_qkv,
    w_attn_out,
):
    vols, tubs, part = tokens.shape
    rows = vols * tubs
    nmp = lax.axis_size(MP)
    nz = lax.axis_size(COLUMN)
    ngroup = lax.axis_size(GROUP)
    dec = w_embed.shape[1]
    feats = dec // nmp
    lists = visible_lists.reshape(1, -1)
    counts = visible_counts.reshape(1, -1)
    slots = lists.shape[1]
    token_row = mask_token.reshape(1, dec)

    own = call(pick_kernel, shape(nmp, 80, 128), lists, counts, tokens.reshape(rows, part))
    full = exchange(own, MP)

    w_q, w_k, w_v = (w_qkv[:, i].reshape(dec, 2, HDIM) for i in range(3))
    w_all = jnp.concatenate(
        [
            jnp.tile(w_q[:, :, None, :], (1, 1, vols, 1)).reshape(dec, 2 * vols * HDIM),
            jnp.concatenate([w_k, w_v], axis=2).reshape(dec, 4 * HDIM),
        ],
        axis=1,
    )
    masked = call(masked_kernel, shape(tubs, 384), token_row, positions, w_all)

    terms = exchange(call(feed_kernel, shape(nmp, 80, 128), full, w_in, w_out), MP)
    embed_parts = exchange(call(embed_kernel, shape(nmp, slots, dec), terms, own, w_embed), MP)
    slot_in, queries, kv = call(
        project_kernel,
        [shape(slots, dec), shape(ngroup, tubs, 128), shape(nz, 80, 128)],
        embed_parts, lists, counts, positions, masked, w_all,
    )
    queries = exchange(queries, GROUP)
    column = exchange(kv, COLUMN)
    start = (lax.axis_index(MP) * feats).reshape(1).astype(I32)
    dec_own = call(
        own_kernel, shape(feats, rows), start, lists, counts, token_row, positions, slot_in, smem=1
    )
    message = call(
        attend_kernel,
        shape(ngroup, 80, 128),
        queries,
        column,
        scratch=[pltpu.VMEM((vols, nz * tubs, 64), BF), pltpu.VMEM((ngroup, 80, 128), F32)],
    )
    message = exchange(message, GROUP)
    head_terms = call(combine_kernel, shape(nmp, feats, rows), message, w_attn_out)
    head_terms = exchange(head_terms, MP)
    return call(finish_kernel, shape(vols, tubs, feats), head_terms, dec_own)


def solution(mesh):
    fine = Mesh(mesh.devices.reshape(8, 2, 4, 4, 2), ("zz", "zp", "y", "x", "core"))
    seq = ("zz", "zp", "y")
    in_specs = (
        P(None, seq, MP),
        P(seq, None, None),
        P(seq, None),
        P(None, MP),
        P(MP, None),
        P(MP, None),
        P(),
        P(seq, None),
        P(None, None, MP),
        P(MP, None),
    )
    out_specs = P(None, seq, MP)
    return jax.shard_map(local, mesh=fine, in_specs=in_specs, out_specs=out_specs, check_vma=False)
```

```python
import functools
import math

import jax
import jax.numpy as jnp
from jax import lax
from jax.experimental import pallas as pl
from jax.experimental.pallas import tpu as pltpu
from jax.sharding import Mesh, PartitionSpec as P

HDIM = 32
MP = ("x", "core")
GROUP = ("zp", "y")
COLUMN = ("zz", "zp")
BF = jnp.bfloat16
F32 = jnp.float32
I32 = jnp.int32


def iota(shape, dim):
    return lax.broadcasted_iota(I32, shape, dim)


def dot(a, b):
    return jnp.dot(a, b, preferred_element_type=F32)


def dot_tn(a, b):
    return lax.dot_general(a, b, (((0,), (0,)), ((), ())), preferred_element_type=F32)


def dot_nt(a, b):
    return lax.dot_general(a, b, (((1,), (1,)), ((), ())), preferred_element_type=F32)


def norm_rows(values):
    mean_row = jnp.mean(values, axis=-1, keepdims=True)
    off = values - mean_row
    spread = jnp.mean(off * off, axis=-1, keepdims=True)
    return off * lax.rsqrt(spread + 1e-05)


def column_of(row):
    n = row.shape[1]
    return jnp.sum(jnp.where(iota((n, n), 0) == iota((n, n), 1), row, 0), axis=1, keepdims=True)


def live_row(lists, counts, rows):
    return jnp.where(counts > 0, lists, rows)


def fold_tail(block):
    tail = block[:, 128:]
    rows = tail.shape[0] // 4
    extra = jnp.concatenate([tail[k * rows : (k + 1) * rows] for k in range(4)], axis=1)
    return jnp.concatenate([block[:, :128], extra], axis=0)


def unfold_tail(folded):
    extra = folded[64:]
    tail = jnp.concatenate([extra[:, 32 * k : 32 * k + 32] for k in range(4)], axis=0)
    return jnp.concatenate([folded[:64], tail], axis=1)


def pick_kernel(lists_hbm, tokens_hbm, out, lists, tokens, sems):
    copies = [
        pltpu.make_async_copy(lists_hbm, lists, sems.at[0]),
        pltpu.make_async_copy(tokens_hbm, tokens, sems.at[1]),
    ]
    for copy in copies:
        copy.start()
    rows = tokens.shape[0]
    copies[0].wait()
    ids = column_of(lists[...])
    named = (ids == iota((ids.shape[0], rows), 1)).astype(F32).astype(BF)
    copies[1].wait()
    own = fold_tail(dot(named, tokens[...])).astype(BF)
    for k in range(out.shape[0]):
        out[k] = own


def feed_kernel(gathered, w_in_hbm, w_out_hbm, out, w_in, w_out, sems):
    copies = [
        pltpu.make_async_copy(w_in_hbm, w_in, sems.at[0]),
        pltpu.make_async_copy(w_out_hbm, w_out, sems.at[1]),
    ]
    for copy in copies:
        copy.start()
    count = gathered.shape[0]
    part = w_in.shape[0] // count
    blocks = [unfold_tail(gathered[k].astype(F32)) for k in range(count)]
    width = count * part
    mean_row = sum(jnp.sum(b, axis=1, keepdims=True) for b in blocks) * (1.0 / width)
    blocks = [b - mean_row for b in blocks]
    spread = sum(jnp.sum(b * b, axis=1, keepdims=True) for b in blocks) * (1.0 / width)
    scale = lax.rsqrt(spread + 1e-05)
    blocks = [(b * scale).astype(BF) for b in blocks]
    copies[0].wait()
    hidden = None
    for k in range(count):
        term = dot(blocks[k], w_in[k * part : (k + 1) * part, :])
        hidden = term if hidden is None else hidden + term
    act = (0.5 * hidden * (1.0 + lax.erf(hidden * math.sqrt(0.5)))).astype(BF)
    copies[1].wait()
    terms = dot(act, w_out[...])
    for k in range(count):
        out[k] = fold_tail(terms[:, k * part : (k + 1) * part]).astype(BF)


def embed_kernel(terms, own, w_embed, out):
    total = own[0].astype(F32) + sum(terms[k].astype(F32) for k in range(terms.shape[0]))
    encoded = unfold_tail(total).astype(BF)
    value = dot(encoded, w_embed[...]).astype(BF)
    for k in range(out.shape[0]):
        out[k] = value


def project_kernel(parts, lists, counts, mask_token, positions, w_rows, slot_in, out):
    tubs = positions.shape[0]
    slots = lists.shape[1]
    ids_row = live_row(lists[...], counts[...], 4 * tubs)
    ids = column_of(ids_row)
    embedded = sum(parts[k].astype(F32) for k in range(parts.shape[0])).astype(BF).astype(F32)
    at = (ids % tubs == iota((slots, tubs), 1)).astype(F32).astype(BF)
    pos = positions[...]
    row_in = (embedded + dot(at, pos)).astype(BF)
    slot_in[...] = row_in
    mask_in = (mask_token[...].astype(F32) + pos.astype(F32)).astype(BF)
    both = jnp.concatenate([mask_in, row_in], axis=0).astype(F32)
    w_q, w_k, w_v = w_rows[0], w_rows[1], w_rows[2]
    heads = [slice(0, HDIM), slice(HDIM, 2 * HDIM)]
    w_all = [w_q[h] for h in heads for _ in range(4)]
    w_all += [w[h] for h in heads for w in (w_k, w_v)]
    w_all = jnp.concatenate(w_all, axis=0)
    both = dot_nt(norm_rows(both).astype(BF), w_all).astype(BF)
    masked, proj = both[:tubs], both[tubs:]

    spot = (ids_row % tubs == iota((tubs, slots), 0)).astype(F32).astype(BF)
    of_volume = ids // tubs == iota((slots, 128), 1) // HDIM
    seen = dot(spot, of_volume.astype(F32).astype(BF)) > 0
    zero = jnp.zeros((slots, 128), BF)
    extra = jnp.concatenate([ids_row.astype(F32), jnp.zeros((1, 128 - slots), F32)], axis=1)
    extra = jnp.broadcast_to(extra, (16, 128)).astype(BF)
    for head in range(2):
        cols = slice(128 * head, 128 * head + 128)
        placed = dot(spot, jnp.where(of_volume, proj[:, cols], zero))
        query = jnp.where(seen, placed, masked[:, cols].astype(F32)).astype(BF)
        cols = slice(256 + 64 * head, 256 + 64 * head + 64)
        block = jnp.concatenate([masked[:, cols], proj[:, cols]], axis=1)
        for k in range(4):
            out[4 * head + k, :tubs] = query
            out[4 * head + k, tubs : 2 * tubs] = block
            out[4 * head + k, 2 * tubs :] = extra


def pair_kernel(start, group, out):
    y = start[0]
    first, second = group.at[y], group.at[4 + y]
    odd = iota((16, 128), 0) % 2 == 1
    ids = jnp.where(odd, second[128:, :].astype(F32), first[128:, :].astype(F32)).astype(BF)
    for k in range(out.shape[0]):
        out[k, :64] = first[64:128, :]
        out[k, 64:128] = second[64:128, :]
        out[k, 128:] = ids


def own_rows(start, lists, counts, mask_token, positions, slot_in, feats, rows):
    tubs, dec = positions.shape
    slots = lists.shape[1]
    ids = column_of(live_row(lists[...], counts[...], rows))
    choose = (iota((dec, feats), 0) == iota((dec, feats), 1) + start).astype(F32).astype(BF)
    mask_in = (mask_token[...].astype(F32) + positions[...].astype(F32)).astype(BF)
    mask_own = dot(mask_in, choose).astype(BF)
    slot_own = dot(slot_in[...], choose).astype(BF)
    picked = (ids == iota((slots, rows), 1)).astype(F32)
    seen = jnp.sum(picked, axis=0, keepdims=True) > 0
    tile = (iota((tubs, rows), 0) == iota((tubs, rows), 1) % tubs).astype(F32).astype(BF)
    return jnp.where(seen, dot_tn(slot_own, picked.astype(BF)), dot_tn(mask_own, tile))


def split_pieces(values, count):
    out = []
    for _ in range(count):
        top = values.astype(BF).astype(F32)
        out.append(top)
        values = values - top
    return out


def attend_kernel(queries, column, out, kv_scr, msg_scr):
    blocks, tubs = queries.shape[0], 64
    nz = 2 * column.shape[0]
    vols = 4
    rows = vols * tubs
    slots = 64
    keys = nz * tubs
    for k in range(nz):
        side = k % 2
        block = column[k // 2, side * tubs : (side + 1) * tubs, :]
        ids_row = column[k // 2, 2 * tubs :, :].astype(F32)[side : side + 1, :slots]
        picked = (ids_row == iota((rows, slots), 0).astype(F32)).astype(F32)
        seen = jnp.sum(picked, axis=1, keepdims=True) > 0
        placed = dot(picked.astype(BF), block[:, 64:])
        other = block[:, :64].astype(F32)
        other = jnp.concatenate([other] * vols, axis=0)
        mat = jnp.where(seen, placed, other).astype(BF)
        for v in range(vols):
            kv_scr[v, k * tubs : (k + 1) * tubs, :] = mat[v * tubs : (v + 1) * tubs]
    packed = queries[:, :tubs, :].reshape(blocks * tubs, 128)
    scale = math.log2(math.e) / math.sqrt(HDIM)
    chunk = 256
    per = chunk // tubs
    for v in range(vols):
        lanes = iota((128, 64), 0)
        take = (lanes == iota((128, 64), 1) + HDIM * v) & (iota((128, 64), 1) < HDIM)
        query = dot(packed, take.astype(F32).astype(BF)).astype(BF)
        kv = kv_scr[v]
        for c in range(blocks // per):
            scores = dot_nt(kv, query[c * chunk : (c + 1) * chunk])
            top = jnp.max(scores, axis=0, keepdims=True)
            weights = jnp.exp2((scores - top) * scale)
            total = jnp.sum(weights, axis=0, keepdims=True)
            summed = dot_tn(kv, weights.astype(BF))[HDIM:]
            stats = jnp.concatenate(
                split_pieces(top * scale, 3) + split_pieces(total, 2) + [jnp.zeros((3, chunk), F32)],
                axis=0,
            )
            side = slice(64 * (v % 2), 64 * (v % 2) + 64)
            for b in range(per):
                cols = slice(b * tubs, (b + 1) * tubs)
                dest = c * per + b
                msg_scr[dest, HDIM * (v // 2) : HDIM * (v // 2) + HDIM, side] = summed[:, cols]
                msg_scr[dest, 64 + 8 * (v // 2) : 72 + 8 * (v // 2), side] = stats[:, cols]
    for b in range(blocks):
        out[b] = msg_scr[b].astype(BF)


def combine_kernel(message, w_attn_out, out):
    ny = 4
    parts = []
    for head in range(2):
        sides = []
        for u in range(2):
            stats = [message[4 * head + k, 64:, :].astype(F32)[8 * u : 8 * u + 8] for k in range(ny)]
            tops = [s[0:1] + s[1:2] + s[2:3] for s in stats]
            best = functools.reduce(jnp.maximum, tops)
            fades = [jnp.exp2(t - best) for t in tops]
            total = sum(f * (s[3:4] + s[4:5]) for f, s in zip(fades, stats))
            value = sum(
                f * message[4 * head + k, HDIM * u : HDIM * u + HDIM, :].astype(F32)
                for k, f in enumerate(fades)
            )
            sides.append(value / total)
        parts.append(jnp.concatenate(sides, axis=1))
    attended = jnp.concatenate(parts, axis=0).astype(BF)
    terms = dot_tn(w_attn_out[...], attended).astype(BF)
    count, feats, rows = out.shape
    for k in range(count):
        out[k] = terms[k * feats : (k + 1) * feats]


def finish_kernel(start, terms, lists, counts, mask_token, positions, slot_in, out):
    vols, tubs, feats = out.shape
    total = own_rows(start[0], lists, counts, mask_token, positions, slot_in, feats, vols * tubs)
    total = total + sum(terms[k].astype(F32) for k in range(terms.shape[0]))
    out[...] = total.T.astype(BF).reshape(vols, tubs, feats)


def call(kernel, out, *args, scratch=(), smem=0, hbm=0):
    specs = [pl.BlockSpec(memory_space=pltpu.SMEM)] * smem
    specs += [pl.BlockSpec(memory_space=pltpu.VMEM)] * (len(args) - smem - hbm)
    specs += [pl.BlockSpec(memory_space=pltpu.HBM)] * hbm
    many = isinstance(out, list)
    one = pl.BlockSpec(memory_space=pltpu.VMEM)
    return pl.pallas_call(
        kernel,
        out_shape=out,
        in_specs=specs,
        out_specs=[one] * len(out) if many else one,
        scratch_shapes=list(scratch),
        compiler_params=pltpu.CompilerParams(vmem_limit_bytes=32 * 2**20),
    )(*args)


def shape(*dims, dtype=BF):
    return jax.ShapeDtypeStruct(dims, dtype)


def exchange(values, axes):
    return lax.all_to_all(values, axes, 0, 0, tiled=True)


def local(
    tokens,
    visible_lists,
    visible_counts,
    w_in,
    w_out,
    w_embed,
    mask_token,
    positions,
    w_qkv,
    w_attn_out,
):
    vols, tubs, part = tokens.shape
    rows = vols * tubs
    nmp = lax.axis_size(MP)
    nz = lax.axis_size(COLUMN)
    ngroup = lax.axis_size(GROUP)
    dec = w_embed.shape[1]
    feats = dec // nmp
    lists = visible_lists.reshape(1, -1)
    counts = visible_counts.reshape(1, -1)
    slots = lists.shape[1]
    token_row = mask_token.reshape(1, dec)
    w_rows = w_qkv.transpose(1, 2, 0)
    pair = pltpu.SemaphoreType.DMA((2,))

    own = call(
        pick_kernel,
        shape(nmp, 80, 128),
        lists,
        tokens.reshape(rows, part),
        hbm=2,
        scratch=[pltpu.VMEM((1, slots), I32), pltpu.VMEM((rows, part), BF), pair],
    )
    full = exchange(own, MP)
    terms = call(
        feed_kernel,
        shape(nmp, 80, 128),
        full,
        w_in,
        w_out,
        hbm=2,
        scratch=[pltpu.VMEM(w_in.shape, BF), pltpu.VMEM(w_out.shape, BF), pair],
    )
    terms = exchange(terms, MP)
    embed_parts = exchange(call(embed_kernel, shape(nmp, slots, dec), terms, own, w_embed), MP)
    slot_in, group = call(
        project_kernel,
        [shape(slots, dec), shape(ngroup, 144, 128)],
        embed_parts, lists, counts, token_row, positions, w_rows,
    )
    group = exchange(group, GROUP)
    y_index = lax.axis_index("y").reshape(1).astype(I32)
    column = call(pair_kernel, shape(lax.axis_size("zz"), 144, 128), y_index, group, smem=1)
    column = exchange(column, "zz")
    message = call(
        attend_kernel,
        shape(ngroup, 80, 128),
        group,
        column,
        scratch=[pltpu.VMEM((vols, nz * tubs, 64), BF), pltpu.VMEM((ngroup, 80, 128), F32)],
    )
    message = exchange(message, GROUP)
    head_terms = call(combine_kernel, shape(nmp, feats, rows), message, w_attn_out)
    head_terms = exchange(head_terms, MP)
    start = (lax.axis_index(MP) * feats).reshape(1).astype(I32)
    return call(
        finish_kernel,
        shape(vols, tubs, feats),
        start, head_terms, lists, counts, token_row, positions, slot_in,
        smem=1,
    )


def solution(mesh):
    fine = Mesh(mesh.devices.reshape(8, 2, 4, 4, 2), ("zz", "zp", "y", "x", "core"))
    seq = ("zz", "zp", "y")
    in_specs = (
        P(None, seq, MP),
        P(seq, None, None),
        P(seq, None),
        P(None, MP),
        P(MP, None),
        P(MP, None),
        P(),
        P(seq, None),
        P(None, None, MP),
        P(MP, None),
    )
    out_specs = P(None, seq, MP)
    return jax.shard_map(local, mesh=fine, in_specs=in_specs, out_specs=out_specs, check_vma=False)
```

```python
import functools
import math

import jax
import jax.numpy as jnp
from jax import lax
from jax.experimental import pallas as pl
from jax.experimental.pallas import tpu as pltpu
from jax.sharding import Mesh, PartitionSpec as P

HDIM = 32
MP = ("x", "core")
GROUP = ("zp", "y")
COLUMN = ("zz", "zp")
BF = jnp.bfloat16
F32 = jnp.float32
I32 = jnp.int32


def iota(shape, dim):
    return lax.broadcasted_iota(I32, shape, dim)


def dot(a, b):
    return jnp.dot(a, b, preferred_element_type=F32)


def dot_tn(a, b):
    return lax.dot_general(a, b, (((0,), (0,)), ((), ())), preferred_element_type=F32)


def dot_nt(a, b):
    return lax.dot_general(a, b, (((1,), (1,)), ((), ())), preferred_element_type=F32)


def norm_rows(values):
    mean_row = jnp.mean(values, axis=-1, keepdims=True)
    off = values - mean_row
    spread = jnp.mean(off * off, axis=-1, keepdims=True)
    return off * lax.rsqrt(spread + 1e-05)


def column_of(row):
    n = row.shape[1]
    return jnp.sum(jnp.where(iota((n, n), 0) == iota((n, n), 1), row, 0), axis=1, keepdims=True)


def live_row(lists, counts, rows):
    return jnp.where(counts > 0, lists, rows)


def fold_tail(block):
    tail = block[:, 128:]
    rows = tail.shape[0] // 4
    extra = jnp.concatenate([tail[k * rows : (k + 1) * rows] for k in range(4)], axis=1)
    return jnp.concatenate([block[:, :128], extra], axis=0)


def unfold_tail(folded):
    extra = folded[64:]
    tail = jnp.concatenate([extra[:, 32 * k : 32 * k + 32] for k in range(4)], axis=0)
    return jnp.concatenate([folded[:64], tail], axis=1)


def pick_kernel(lists_hbm, tokens_hbm, out, lists, tokens, sems):
    copies = [
        pltpu.make_async_copy(lists_hbm, lists, sems.at[0]),
        pltpu.make_async_copy(tokens_hbm, tokens, sems.at[1]),
    ]
    for copy in copies:
        copy.start()
    rows = tokens.shape[0]
    copies[0].wait()
    ids = column_of(lists[...])
    named = (ids == iota((ids.shape[0], rows), 1)).astype(F32).astype(BF)
    copies[1].wait()
    own = fold_tail(dot(named, tokens[...])).astype(BF)
    for k in range(out.shape[0]):
        out[k] = own


def feed_kernel(gathered, w_in_hbm, w_out_hbm, out, w_in, w_out, sems):
    copies = [
        pltpu.make_async_copy(w_in_hbm, w_in, sems.at[0]),
        pltpu.make_async_copy(w_out_hbm, w_out, sems.at[1]),
    ]
    for copy in copies:
        copy.start()
    count = gathered.shape[0]
    part = w_in.shape[0] // count
    blocks = [unfold_tail(gathered[k].astype(F32)) for k in range(count)]
    width = count * part
    mean_row = sum(jnp.sum(b, axis=1, keepdims=True) for b in blocks) * (1.0 / width)
    blocks = [b - mean_row for b in blocks]
    spread = sum(jnp.sum(b * b, axis=1, keepdims=True) for b in blocks) * (1.0 / width)
    scale = lax.rsqrt(spread + 1e-05)
    blocks = [(b * scale).astype(BF) for b in blocks]
    copies[0].wait()
    hidden = None
    for k in range(count):
        term = dot(blocks[k], w_in[k * part : (k + 1) * part, :])
        hidden = term if hidden is None else hidden + term
    act = (0.5 * hidden * (1.0 + lax.erf(hidden * math.sqrt(0.5)))).astype(BF)
    copies[1].wait()
    terms = dot(act, w_out[...])
    for k in range(count):
        out[k] = fold_tail(terms[:, k * part : (k + 1) * part]).astype(BF)


def embed_kernel(terms, own, w_embed, out):
    total = own[0].astype(F32) + sum(terms[k].astype(F32) for k in range(terms.shape[0]))
    encoded = unfold_tail(total).astype(BF)
    value = dot(encoded, w_embed[...]).astype(BF)
    for k in range(out.shape[0]):
        out[k] = value


def project_kernel(parts, lists, counts, mask_token, positions, w_rows, slot_in, out):
    tubs = positions.shape[0]
    slots = lists.shape[1]
    ids_row = live_row(lists[...], counts[...], 4 * tubs)
    ids = column_of(ids_row)
    embedded = sum(parts[k].astype(F32) for k in range(parts.shape[0])).astype(BF).astype(F32)
    at = (ids % tubs == iota((slots, tubs), 1)).astype(F32).astype(BF)
    pos = positions[...]
    row_in = (embedded + dot(at, pos)).astype(BF)
    slot_in[...] = row_in
    mask_in = (mask_token[...].astype(F32).reshape(1, -1) + pos.astype(F32)).astype(BF)
    both = jnp.concatenate([mask_in, row_in], axis=0).astype(F32)
    w_q, w_k, w_v = w_rows[0], w_rows[1], w_rows[2]
    heads = [slice(0, HDIM), slice(HDIM, 2 * HDIM)]
    w_all = [w_q[h] for h in heads for _ in range(4)]
    w_all += [w[h] for h in heads for w in (w_k, w_v)]
    w_all = jnp.concatenate(w_all, axis=0)
    both = dot_nt(norm_rows(both).astype(BF), w_all).astype(BF)
    masked, proj = both[:tubs], both[tubs:]

    spot = (ids_row % tubs == iota((tubs, slots), 0)).astype(F32).astype(BF)
    of_volume = ids // tubs == iota((slots, 128), 1) // HDIM
    seen = dot(spot, of_volume.astype(F32).astype(BF)) > 0
    zero = jnp.zeros((slots, 128), BF)
    extra = jnp.concatenate([ids_row.astype(F32), jnp.zeros((1, 128 - slots), F32)], axis=1)
    extra = jnp.broadcast_to(extra, (16, 128)).astype(BF)
    for head in range(2):
        cols = slice(128 * head, 128 * head + 128)
        placed = dot(spot, jnp.where(of_volume, proj[:, cols], zero))
        query = jnp.where(seen, placed, masked[:, cols].astype(F32)).astype(BF)
        cols = slice(256 + 64 * head, 256 + 64 * head + 64)
        block = jnp.concatenate([masked[:, cols], proj[:, cols]], axis=1)
        for k in range(4):
            out[4 * head + k, :tubs] = query
            out[4 * head + k, tubs : 2 * tubs] = block
            out[4 * head + k, 2 * tubs :] = extra


def pair_kernel(group, out):
    y = lax.axis_index("y")
    first, second = group.at[y], group.at[4 + y]
    odd = iota((16, 128), 0) % 2 == 1
    ids = jnp.where(odd, second[128:, :].astype(F32), first[128:, :].astype(F32)).astype(BF)
    for k in range(out.shape[0]):
        out[k, :64] = first[64:128, :]
        out[k, 64:128] = second[64:128, :]
        out[k, 128:] = ids


def own_rows(start, lists, counts, mask_token, positions, slot_in, feats, rows):
    tubs, dec = positions.shape
    slots = lists.shape[1]
    ids = column_of(live_row(lists[...], counts[...], rows))
    choose = (iota((dec, feats), 0) == iota((dec, feats), 1) + start).astype(F32).astype(BF)
    mask_in = (mask_token[...].astype(F32).reshape(1, -1) + positions[...].astype(F32)).astype(BF)
    mask_own = dot(mask_in, choose).astype(BF)
    slot_own = dot(slot_in[...], choose).astype(BF)
    picked = (ids == iota((slots, rows), 1)).astype(F32)
    seen = jnp.sum(picked, axis=0, keepdims=True) > 0
    tile = (iota((tubs, rows), 0) == iota((tubs, rows), 1) % tubs).astype(F32).astype(BF)
    return jnp.where(seen, dot_tn(slot_own, picked.astype(BF)), dot_tn(mask_own, tile))


def split_pieces(values, count):
    out = []
    for _ in range(count):
        top = values.astype(BF).astype(F32)
        out.append(top)
        values = values - top
    return out


def attend_kernel(queries, column, out, kv_scr, msg_scr):
    blocks, tubs = queries.shape[0], 64
    nz = 2 * column.shape[0]
    vols = 4
    rows = vols * tubs
    slots = 64
    keys = nz * tubs
    for k in range(nz):
        side = k % 2
        block = column[k // 2, side * tubs : (side + 1) * tubs, :]
        ids_row = column[k // 2, 2 * tubs :, :].astype(F32)[side : side + 1, :slots]
        picked = (ids_row == iota((rows, slots), 0).astype(F32)).astype(F32)
        seen = jnp.sum(picked, axis=1, keepdims=True) > 0
        placed = dot(picked.astype(BF), block[:, 64:])
        other = block[:, :64].astype(F32)
        other = jnp.concatenate([other] * vols, axis=0)
        mat = jnp.where(seen, placed, other).astype(BF)
        for v in range(vols):
            kv_scr[v, k * tubs : (k + 1) * tubs, :] = mat[v * tubs : (v + 1) * tubs]
    packed = queries[:, :tubs, :].reshape(blocks * tubs, 128)
    scale = math.log2(math.e) / math.sqrt(HDIM)

    def score(v):
        take = (iota((128, 64), 0) == iota((128, 64), 1) + HDIM * v) & (iota((128, 64), 1) < HDIM)
        query = dot(packed, take.astype(F32).astype(BF)).astype(BF)
        return dot_nt(kv_scr[v], query)

    def weigh(scores):
        top = jnp.max(scores, axis=0, keepdims=True)
        weights = jnp.exp2((scores - top) * scale)
        return top, jnp.sum(weights, axis=0, keepdims=True), weights.astype(BF)

    def put(v, top, total, weights):
        summed = dot_tn(kv_scr[v], weights)[HDIM:]
        stats = split_pieces(top * scale, 3) + split_pieces(total, 2)
        stats = jnp.concatenate(stats + [jnp.zeros((3, blocks * tubs), F32)], axis=0)
        half, side = v // 2, slice(64 * (v % 2), 64 * (v % 2) + 64)
        for b in range(blocks):
            cols = slice(b * tubs, (b + 1) * tubs)
            msg_scr[b, HDIM * half : HDIM * half + HDIM, side] = summed[:, cols]
            msg_scr[b, 64 + 8 * half : 72 + 8 * half, side] = stats[:, cols]

    scores, waiting = score(0), None
    for v in range(vols):
        later = score(v + 1) if v + 1 < vols else None
        weighed = weigh(scores)
        if waiting is not None:
            put(*waiting)
        waiting, scores = (v, *weighed), later
    put(*waiting)
    for b in range(blocks):
        out[b] = msg_scr[b].astype(BF)


def combine_kernel(message, w_attn_out, out):
    ny = 4
    parts = []
    for head in range(2):
        sides = []
        for u in range(2):
            stats = [message[4 * head + k, 64:, :].astype(F32)[8 * u : 8 * u + 8] for k in range(ny)]
            tops = [s[0:1] + s[1:2] + s[2:3] for s in stats]
            best = functools.reduce(jnp.maximum, tops)
            fades = [jnp.exp2(t - best) for t in tops]
            total = sum(f * (s[3:4] + s[4:5]) for f, s in zip(fades, stats))
            value = sum(
                f * message[4 * head + k, HDIM * u : HDIM * u + HDIM, :].astype(F32)
                for k, f in enumerate(fades)
            )
            sides.append(value / total)
        parts.append(jnp.concatenate(sides, axis=1))
    attended = jnp.concatenate(parts, axis=0).astype(BF)
    terms = dot_tn(w_attn_out[...], attended).astype(BF)
    count, feats, rows = out.shape
    for k in range(count):
        out[k] = terms[k * feats : (k + 1) * feats]


def finish_kernel(terms, lists, counts, mask_token, positions, slot_in, out):
    vols, tubs, feats = out.shape
    start = lax.axis_index(MP) * feats
    total = own_rows(start, lists, counts, mask_token, positions, slot_in, feats, vols * tubs)
    total = total + sum(terms[k].astype(F32) for k in range(terms.shape[0]))
    out[...] = total.T.astype(BF).reshape(vols, tubs, feats)


def call(kernel, out, *args, scratch=(), hbm=0):
    specs = [pl.BlockSpec(memory_space=pltpu.VMEM)] * (len(args) - hbm)
    specs += [pl.BlockSpec(memory_space=pl.ANY)] * hbm
    many = isinstance(out, list)
    one = pl.BlockSpec(memory_space=pltpu.VMEM)
    return pl.pallas_call(
        kernel,
        out_shape=out,
        in_specs=specs,
        out_specs=[one] * len(out) if many else one,
        scratch_shapes=list(scratch),
        compiler_params=None if hbm else pltpu.CompilerParams(vmem_limit_bytes=32 * 2**20),
    )(*args)


def shape(*dims, dtype=BF):
    return jax.ShapeDtypeStruct(dims, dtype)


def exchange(values, axes):
    return lax.all_to_all(values, axes, 0, 0, tiled=True)


def local(
    tokens,
    visible_lists,
    visible_counts,
    w_in,
    w_out,
    w_embed,
    mask_token,
    positions,
    w_qkv,
    w_attn_out,
):
    vols, tubs, part = tokens.shape
    rows = vols * tubs
    nmp = lax.axis_size(MP)
    nz = lax.axis_size(COLUMN)
    ngroup = lax.axis_size(GROUP)
    dec = w_embed.shape[1]
    feats = dec // nmp
    lists = visible_lists.reshape(1, -1)
    counts = visible_counts.reshape(1, -1)
    slots = lists.shape[1]
    w_rows = w_qkv.transpose(1, 2, 0)
    pair = pltpu.SemaphoreType.DMA((2,))

    own = call(
        pick_kernel,
        shape(nmp, 80, 128),
        lists,
        tokens.reshape(rows, part),
        hbm=2,
        scratch=[pltpu.VMEM((1, slots), I32), pltpu.VMEM((rows, part), BF), pair],
    )
    full = exchange(own, MP)
    terms = call(
        feed_kernel,
        shape(nmp, 80, 128),
        full,
        w_in,
        w_out,
        hbm=2,
        scratch=[pltpu.VMEM(w_in.shape, BF), pltpu.VMEM(w_out.shape, BF), pair],
    )
    terms = exchange(terms, MP)
    embed_parts = exchange(call(embed_kernel, shape(nmp, slots, dec), terms, own, w_embed), MP)
    slot_in, group = call(
        project_kernel,
        [shape(slots, dec), shape(ngroup, 144, 128)],
        embed_parts, lists, counts, mask_token, positions, w_rows,
    )
    group = exchange(group, GROUP)
    column = call(pair_kernel, shape(lax.axis_size("zz"), 144, 128), group)
    column = exchange(column, "zz")
    message = call(
        attend_kernel,
        shape(ngroup, 80, 128),
        group,
        column,
        scratch=[pltpu.VMEM((vols, nz * tubs, 64), BF), pltpu.VMEM((ngroup, 80, 128), F32)],
    )
    message = exchange(message, GROUP)
    head_terms = call(combine_kernel, shape(nmp, feats, rows), message, w_attn_out)
    head_terms = exchange(head_terms, MP)
    return call(
        finish_kernel,
        shape(vols, tubs, feats),
        head_terms, lists, counts, mask_token, positions, slot_in,
    )


def solution(mesh):
    fine = Mesh(mesh.devices.reshape(8, 2, 4, 4, 2), ("zz", "zp", "y", "x", "core"))
    seq = ("zz", "zp", "y")
    in_specs = (
        P(None, seq, MP),
        P(seq, None, None),
        P(seq, None),
        P(None, MP),
        P(MP, None),
        P(MP, None),
        P(),
        P(seq, None),
        P(None, None, MP),
        P(MP, None),
    )
    out_specs = P(None, seq, MP)
    return jax.shard_map(local, mesh=fine, in_specs=in_specs, out_specs=out_specs, check_vma=False)
```

```python
import functools
import math

import jax
import jax.numpy as jnp
from jax import lax
from jax.experimental import pallas as pl
from jax.experimental.pallas import tpu as pltpu
from jax.sharding import Mesh, PartitionSpec as P

HDIM = 32
MP = ("x", "core")
GROUP = ("zp", "y")
COLUMN = ("zz", "zp")
BF = jnp.bfloat16
F32 = jnp.float32
I32 = jnp.int32


def iota(shape, dim):
    return lax.broadcasted_iota(I32, shape, dim)


def dot(a, b):
    return jnp.dot(a, b, preferred_element_type=F32)


def dot_tn(a, b):
    return lax.dot_general(a, b, (((0,), (0,)), ((), ())), preferred_element_type=F32)


def dot_nt(a, b):
    return lax.dot_general(a, b, (((1,), (1,)), ((), ())), preferred_element_type=F32)


def norm_rows(values):
    mean_row = jnp.mean(values, axis=-1, keepdims=True)
    off = values - mean_row
    spread = jnp.mean(off * off, axis=-1, keepdims=True)
    return off * lax.rsqrt(spread + 1e-05)


def column_of(row):
    n = row.shape[1]
    return jnp.sum(jnp.where(iota((n, n), 0) == iota((n, n), 1), row, 0), axis=1, keepdims=True)


def live_row(lists, counts, rows):
    return jnp.where(counts > 0, lists, rows)


def fold_tail(block):
    tail = block[:, 128:]
    rows = tail.shape[0] // 4
    extra = jnp.concatenate([tail[k * rows : (k + 1) * rows] for k in range(4)], axis=1)
    return jnp.concatenate([block[:, :128], extra], axis=0)


def unfold_tail(folded):
    extra = folded[64:]
    tail = jnp.concatenate([extra[:, 32 * k : 32 * k + 32] for k in range(4)], axis=0)
    return jnp.concatenate([folded[:64], tail], axis=1)


def pick_kernel(lists, tokens, out):
    rows = tokens.shape[0]
    ids = column_of(lists[...])
    named = (ids == iota((ids.shape[0], rows), 1)).astype(F32).astype(BF)
    own = fold_tail(dot(named, tokens[...])).astype(BF)
    for k in range(out.shape[0]):
        out[k] = own


def feed_kernel(gathered, w_in, w_out, out):
    count = gathered.shape[0]
    part = w_in.shape[0] // count
    blocks = [unfold_tail(gathered[k].astype(F32)) for k in range(count)]
    width = count * part
    mean_row = sum(jnp.sum(b, axis=1, keepdims=True) for b in blocks) * (1.0 / width)
    blocks = [b - mean_row for b in blocks]
    spread = sum(jnp.sum(b * b, axis=1, keepdims=True) for b in blocks) * (1.0 / width)
    scale = lax.rsqrt(spread + 1e-05)
    hidden = None
    for k in range(count):
        term = dot((blocks[k] * scale).astype(BF), w_in[k * part : (k + 1) * part, :])
        hidden = term if hidden is None else hidden + term
    act = (0.5 * hidden * (1.0 + lax.erf(hidden * math.sqrt(0.5)))).astype(BF)
    terms = dot(act, w_out[...])
    for k in range(count):
        out[k] = fold_tail(terms[:, k * part : (k + 1) * part]).astype(BF)


def embed_kernel(terms, own, w_embed, out):
    total = own[0].astype(F32) + sum(terms[k].astype(F32) for k in range(terms.shape[0]))
    encoded = unfold_tail(total).astype(BF)
    value = dot(encoded, w_embed[...]).astype(BF)
    for k in range(out.shape[0]):
        out[k] = value


def project_kernel(parts, lists, counts, mask_token, positions, w_rows, slot_in, out):
    tubs = positions.shape[0]
    slots = lists.shape[1]
    ids_row = live_row(lists[...], counts[...], 4 * tubs)
    ids = column_of(ids_row)
    embedded = sum(parts[k].astype(F32) for k in range(parts.shape[0])).astype(BF).astype(F32)
    at = (ids % tubs == iota((slots, tubs), 1)).astype(F32).astype(BF)
    pos = positions[...]
    row_in = (embedded + dot(at, pos)).astype(BF)
    slot_in[...] = row_in
    mask_in = (mask_token[...].astype(F32).reshape(1, -1) + pos.astype(F32)).astype(BF)
    both = jnp.concatenate([mask_in, row_in], axis=0).astype(F32)
    w_q, w_k, w_v = w_rows[0], w_rows[1], w_rows[2]
    heads = [slice(0, HDIM), slice(HDIM, 2 * HDIM)]
    w_all = [w_q[h] for h in heads for _ in range(4)]
    w_all += [w[h] for h in heads for w in (w_k, w_v)]
    w_all = jnp.concatenate(w_all, axis=0)
    both = dot_nt(norm_rows(both).astype(BF), w_all).astype(BF)
    masked, proj = both[:tubs], both[tubs:]

    spot = (ids_row % tubs == iota((tubs, slots), 0)).astype(F32).astype(BF)
    of_volume = ids // tubs == iota((slots, 128), 1) // HDIM
    seen = dot(spot, of_volume.astype(F32).astype(BF)) > 0
    zero = jnp.zeros((slots, 128), BF)
    extra = jnp.concatenate([ids_row.astype(F32), jnp.zeros((1, 128 - slots), F32)], axis=1)
    extra = jnp.broadcast_to(extra, (16, 128)).astype(BF)
    for head in range(2):
        cols = slice(128 * head, 128 * head + 128)
        placed = dot(spot, jnp.where(of_volume, proj[:, cols], zero))
        query = jnp.where(seen, placed, masked[:, cols].astype(F32)).astype(BF)
        cols = slice(256 + 64 * head, 256 + 64 * head + 64)
        block = jnp.concatenate([masked[:, cols], proj[:, cols]], axis=1)
        for k in range(4):
            out[4 * head + k, :tubs] = query
            out[4 * head + k, tubs : 2 * tubs] = block
            out[4 * head + k, 2 * tubs :] = extra


def pair_kernel(group, out):
    y = lax.axis_index("y")
    first, second = group.at[y], group.at[4 + y]
    odd = iota((16, 128), 0) % 2 == 1
    ids = jnp.where(odd, second[128:, :].astype(F32), first[128:, :].astype(F32)).astype(BF)
    for k in range(out.shape[0]):
        out[k, :64] = first[64:128, :]
        out[k, 64:128] = second[64:128, :]
        out[k, 128:] = ids


def own_rows(start, lists, counts, mask_token, positions, slot_in, feats, rows):
    tubs, dec = positions.shape
    slots = lists.shape[1]
    ids = column_of(live_row(lists[...], counts[...], rows))
    choose = (iota((dec, feats), 0) == iota((dec, feats), 1) + start).astype(F32).astype(BF)
    mask_in = (mask_token[...].astype(F32).reshape(1, -1) + positions[...].astype(F32)).astype(BF)
    mask_own = dot(mask_in, choose).astype(BF)
    slot_own = dot(slot_in[...], choose).astype(BF)
    picked = (ids == iota((slots, rows), 1)).astype(F32)
    seen = jnp.sum(picked, axis=0, keepdims=True) > 0
    tile = (iota((tubs, rows), 0) == iota((tubs, rows), 1) % tubs).astype(F32).astype(BF)
    return jnp.where(seen, dot_tn(slot_own, picked.astype(BF)), dot_tn(mask_own, tile))


def split_pieces(values, count):
    out = []
    for _ in range(count):
        top = values.astype(BF).astype(F32)
        out.append(top)
        values = values - top
    return out


def attend_kernel(queries, column, out, kv_scr, msg_scr):
    blocks, tubs = queries.shape[0], 64
    nz = 2 * column.shape[0]
    vols = 4
    rows = vols * tubs
    slots = 64
    keys = nz * tubs
    for k in range(nz):
        side = k % 2
        block = column[k // 2, side * tubs : (side + 1) * tubs, :]
        ids_row = column[k // 2, 2 * tubs :, :].astype(F32)[side : side + 1, :slots]
        picked = (ids_row == iota((rows, slots), 0).astype(F32)).astype(F32)
        seen = jnp.sum(picked, axis=1, keepdims=True) > 0
        placed = dot(picked.astype(BF), block[:, 64:])
        other = block[:, :64].astype(F32)
        other = jnp.concatenate([other] * vols, axis=0)
        mat = jnp.where(seen, placed, other).astype(BF)
        for v in range(vols):
            kv_scr[v, k * tubs : (k + 1) * tubs, :] = mat[v * tubs : (v + 1) * tubs]
    packed = queries[:, :tubs, :].reshape(blocks * tubs, 128)
    scale = math.log2(math.e) / math.sqrt(HDIM)

    def score(v):
        take = (iota((128, 64), 0) == iota((128, 64), 1) + HDIM * v) & (iota((128, 64), 1) < HDIM)
        query = dot(packed, take.astype(F32).astype(BF)).astype(BF)
        return dot_nt(kv_scr[v], query)

    def weigh(scores):
        top = jnp.max(scores, axis=0, keepdims=True)
        weights = jnp.exp2((scores - top) * scale)
        return top, jnp.sum(weights, axis=0, keepdims=True), weights.astype(BF)

    def put(v, top, total, weights):
        summed = dot_tn(kv_scr[v], weights)[HDIM:]
        stats = split_pieces(top * scale, 3) + split_pieces(total, 2)
        stats = jnp.concatenate(stats + [jnp.zeros((3, blocks * tubs), F32)], axis=0)
        half, side = v // 2, slice(64 * (v % 2), 64 * (v % 2) + 64)
        for b in range(blocks):
            cols = slice(b * tubs, (b + 1) * tubs)
            msg_scr[b, HDIM * half : HDIM * half + HDIM, side] = summed[:, cols]
            msg_scr[b, 64 + 8 * half : 72 + 8 * half, side] = stats[:, cols]

    scores, waiting = score(0), None
    for v in range(vols):
        later = score(v + 1) if v + 1 < vols else None
        weighed = weigh(scores)
        if waiting is not None:
            put(*waiting)
        waiting, scores = (v, *weighed), later
    put(*waiting)
    for b in range(blocks):
        out[b] = msg_scr[b].astype(BF)


def combine_kernel(message, w_attn_out, out):
    ny = 4
    parts = []
    for head in range(2):
        sides = []
        for u in range(2):
            stats = [message[4 * head + k, 64:, :].astype(F32)[8 * u : 8 * u + 8] for k in range(ny)]
            tops = [s[0:1] + s[1:2] + s[2:3] for s in stats]
            best = functools.reduce(jnp.maximum, tops)
            fades = [jnp.exp2(t - best) for t in tops]
            total = sum(f * (s[3:4] + s[4:5]) for f, s in zip(fades, stats))
            value = sum(
                f * message[4 * head + k, HDIM * u : HDIM * u + HDIM, :].astype(F32)
                for k, f in enumerate(fades)
            )
            sides.append(value / total)
        parts.append(jnp.concatenate(sides, axis=1))
    attended = jnp.concatenate(parts, axis=0).astype(BF)
    terms = dot_tn(w_attn_out[...], attended).astype(BF)
    count, feats, rows = out.shape
    for k in range(count):
        out[k] = terms[k * feats : (k + 1) * feats]


def finish_kernel(terms, lists, counts, mask_token, positions, slot_in, out):
    vols, tubs, feats = out.shape
    start = lax.axis_index(MP) * feats
    total = own_rows(start, lists, counts, mask_token, positions, slot_in, feats, vols * tubs)
    total = total + sum(terms[k].astype(F32) for k in range(terms.shape[0]))
    out[...] = total.T.astype(BF).reshape(vols, tubs, feats)


def call(kernel, out, *args, scratch=(), micros=0):
    many = isinstance(out, list)
    one = pl.BlockSpec(memory_space=pltpu.VMEM)
    cost = None
    if micros:
        cost = pl.CostEstimate(
            flops=micros * 10**9, bytes_accessed=micros * 10**6, transcendentals=0
        )
    return pl.pallas_call(
        kernel,
        out_shape=out,
        in_specs=[one] * len(args),
        out_specs=[one] * len(out) if many else one,
        scratch_shapes=list(scratch),
        compiler_params=pltpu.CompilerParams(vmem_limit_bytes=32 * 2**20),
        cost_estimate=cost,
    )(*args)


def shape(*dims, dtype=BF):
    return jax.ShapeDtypeStruct(dims, dtype)


def exchange(values, axes):
    return lax.all_to_all(values, axes, 0, 0, tiled=True)


def local(
    tokens,
    visible_lists,
    visible_counts,
    w_in,
    w_out,
    w_embed,
    mask_token,
    positions,
    w_qkv,
    w_attn_out,
):
    vols, tubs, part = tokens.shape
    rows = vols * tubs
    nmp = lax.axis_size(MP)
    nz = lax.axis_size(COLUMN)
    ngroup = lax.axis_size(GROUP)
    dec = w_embed.shape[1]
    feats = dec // nmp
    lists = visible_lists.reshape(1, -1)
    counts = visible_counts.reshape(1, -1)
    slots = lists.shape[1]
    w_rows = w_qkv.transpose(1, 2, 0)

    own = call(
        pick_kernel, shape(nmp, 80, 128), lists, tokens.reshape(rows, part), micros=10
    )
    full = exchange(own, MP)
    terms = call(feed_kernel, shape(nmp, 80, 128), full, w_in, w_out)
    terms = exchange(terms, MP)
    embed_parts = exchange(call(embed_kernel, shape(nmp, slots, dec), terms, own, w_embed), MP)
    slot_in, group = call(
        project_kernel,
        [shape(slots, dec), shape(ngroup, 144, 128)],
        embed_parts, lists, counts, mask_token, positions, w_rows,
    )
    group = exchange(group, GROUP)
    column = call(pair_kernel, shape(lax.axis_size("zz"), 144, 128), group)
    column = exchange(column, "zz")
    message = call(
        attend_kernel,
        shape(ngroup, 80, 128),
        group,
        column,
        scratch=[pltpu.VMEM((vols, nz * tubs, 64), BF), pltpu.VMEM((ngroup, 80, 128), F32)],
    )
    message = exchange(message, GROUP)
    head_terms = call(combine_kernel, shape(nmp, feats, rows), message, w_attn_out)
    head_terms = exchange(head_terms, MP)
    return call(
        finish_kernel,
        shape(vols, tubs, feats),
        head_terms, lists, counts, mask_token, positions, slot_in,
    )


def solution(mesh):
    fine = Mesh(mesh.devices.reshape(8, 2, 4, 4, 2), ("zz", "zp", "y", "x", "core"))
    seq = ("zz", "zp", "y")
    in_specs = (
        P(None, seq, MP),
        P(seq, None, None),
        P(seq, None),
        P(None, MP),
        P(MP, None),
        P(MP, None),
        P(),
        P(seq, None),
        P(None, None, MP),
        P(MP, None),
    )
    out_specs = P(None, seq, MP)
    return jax.shard_map(local, mesh=fine, in_specs=in_specs, out_specs=out_specs, check_vma=False)
```

```python
import functools
import math

import jax
import jax.numpy as jnp
from jax import lax
from jax.experimental import pallas as pl
from jax.experimental.pallas import tpu as pltpu
from jax.sharding import PartitionSpec as P

HDIM = 32
NY = 4
NZ = 16
GROUP = [[(2 * k + p) * NY + y for p in range(2) for y in range(NY)] for k in range(NZ // 2)]
COLUMN = [
    [z * NY + y for z in range(NZ) if (z + z // (NZ // 2)) % 2 == head]
    for head in range(2)
    for y in range(NY)
]
ALONG_X = [[0, 2, 4, 6], [1, 3, 5, 7]]
CORES = [[0, 1], [2, 3], [4, 5], [6, 7]]
BF = jnp.bfloat16
F32 = jnp.float32
I32 = jnp.int32


def iota(shape, dim):
    return lax.broadcasted_iota(I32, shape, dim)


def dot(a, b):
    return jnp.dot(a, b, preferred_element_type=F32)


def dot_tn(a, b):
    return lax.dot_general(a, b, (((0,), (0,)), ((), ())), preferred_element_type=F32)


def dot_nt(a, b):
    return lax.dot_general(a, b, (((1,), (1,)), ((), ())), preferred_element_type=F32)


def norm_rows(values):
    mean_row = jnp.mean(values, axis=-1, keepdims=True)
    off = values - mean_row
    spread = jnp.mean(off * off, axis=-1, keepdims=True)
    return off * lax.rsqrt(spread + 1e-05)


def column_of(row):
    n = row.shape[1]
    return jnp.sum(jnp.where(iota((n, n), 0) == iota((n, n), 1), row, 0), axis=1, keepdims=True)


def plane_turn():
    return lax.axis_index("seq") // (NY * NZ // 2)


def live_row(lists, counts, rows):
    return jnp.where(counts > 0, lists, rows)


def fold_tail(block):
    tail = block[:, 128:]
    rows = tail.shape[0] // 4
    extra = jnp.concatenate([tail[k * rows : (k + 1) * rows] for k in range(4)], axis=1)
    return jnp.concatenate([block[:, :128], extra], axis=0)


def unfold_tail(folded):
    extra = folded[64:]
    tail = jnp.concatenate([extra[:, 32 * k : 32 * k + 32] for k in range(4)], axis=0)
    return jnp.concatenate([folded[:64], tail], axis=1)


def pick_kernel(lists, tokens, out):
    rows = tokens.shape[0]
    ids = column_of(lists[...])
    named = (ids == iota((ids.shape[0], rows), 1)).astype(F32).astype(BF)
    own = fold_tail(dot(named, tokens[...])).astype(BF)
    for k in range(out.shape[0]):
        out[k] = own


def feed_kernel(gathered, w_in, w_out, out):
    count = gathered.shape[0]
    part = w_in.shape[0] // count
    blocks = [unfold_tail(gathered[k].astype(F32)) for k in range(count)]
    width = count * part
    mean_row = sum(jnp.sum(b, axis=1, keepdims=True) for b in blocks) * (1.0 / width)
    blocks = [b - mean_row for b in blocks]
    spread = sum(jnp.sum(b * b, axis=1, keepdims=True) for b in blocks) * (1.0 / width)
    scale = lax.rsqrt(spread + 1e-05)
    hidden = None
    for k in range(count):
        term = dot((blocks[k] * scale).astype(BF), w_in[k * part : (k + 1) * part, :])
        hidden = term if hidden is None else hidden + term
    act = (0.5 * hidden * (1.0 + lax.erf(hidden * math.sqrt(0.5)))).astype(BF)
    terms = dot(act, w_out[...])
    for k in range(count):
        out[k] = fold_tail(terms[:, k * part : (k + 1) * part]).astype(BF)


def embed_kernel(terms, own, w_embed, out):
    total = own[0].astype(F32) + sum(terms[k].astype(F32) for k in range(terms.shape[0]))
    encoded = unfold_tail(total).astype(BF)
    value = dot(encoded, w_embed[...]).astype(BF)
    for k in range(out.shape[0]):
        out[k] = value


def join_kernel(parts, out):
    out[...] = sum(parts[k].astype(F32) for k in range(parts.shape[0]))


def project_kernel(parts, lists, counts, mask_token, positions, w_rows, slot_in, out):
    tubs = positions.shape[0]
    slots = lists.shape[1]
    ids_row = live_row(lists[...], counts[...], 4 * tubs)
    ids = column_of(ids_row)
    embedded = sum(parts[k] for k in range(parts.shape[0])).astype(BF).astype(F32)
    at = (ids % tubs == iota((slots, tubs), 1)).astype(F32).astype(BF)
    pos = positions[...]
    row_in = (embedded + dot(at, pos)).astype(BF)
    slot_in[...] = row_in
    mask_in = (mask_token[...].astype(F32).reshape(1, -1) + pos.astype(F32)).astype(BF)
    both = jnp.concatenate([mask_in, row_in], axis=0).astype(F32)
    w_q, w_k, w_v = w_rows[0], w_rows[1], w_rows[2]
    heads = [slice(0, HDIM), slice(HDIM, 2 * HDIM)]
    w_all = [w_q[h] for h in heads for _ in range(4)]
    w_all += [w[h] for h in heads for w in (w_k, w_v)]
    w_all = jnp.concatenate(w_all, axis=0)
    both = dot_nt(norm_rows(both).astype(BF), w_all).astype(BF)
    masked, proj = both[:tubs], both[tubs:]

    spot = (ids_row % tubs == iota((tubs, slots), 0)).astype(F32).astype(BF)
    of_volume = ids // tubs == iota((slots, 128), 1) // HDIM
    seen = dot(spot, of_volume.astype(F32).astype(BF)) > 0
    zero = jnp.zeros((slots, 128), BF)
    extra = jnp.concatenate([ids_row.astype(F32), jnp.zeros((1, 128 - slots), F32)], axis=1)
    extra = jnp.broadcast_to(extra, (8, 128)).astype(BF)
    turn = plane_turn()
    for head in range(2):
        cols = slice(128 * head, 128 * head + 128)
        placed = dot(spot, jnp.where(of_volume, proj[:, cols], zero))
        query = jnp.where(seen, placed, masked[:, cols].astype(F32)).astype(BF)
        cols = slice(256 + 64 * head, 256 + 64 * head + 64)
        block = jnp.concatenate([masked[:, cols], proj[:, cols]], axis=1)
        block = jnp.concatenate([query, block, extra], axis=0)
        plane = jnp.where(turn == 0, head, 1 - head)
        for k in range(NY):
            out[NY * plane + k] = block


def pair_kernel(group, out):
    y = lax.axis_index("seq") % NY
    first, second = group[y], group[NY + y]
    odd = iota((8, 128), 0) % 2 == 1
    ids = jnp.where(odd, second[128:].astype(F32), first[128:].astype(F32)).astype(BF)
    block = jnp.concatenate([first[64:128], second[64:128], ids], axis=0)
    for k in range(out.shape[0]):
        out[k] = block


def own_rows(start, lists, counts, mask_token, positions, slot_in, feats, rows):
    tubs, dec = positions.shape
    slots = lists.shape[1]
    ids = column_of(live_row(lists[...], counts[...], rows))
    choose = (iota((dec, feats), 0) == iota((dec, feats), 1) + start).astype(F32).astype(BF)
    mask_in = (mask_token[...].astype(F32).reshape(1, -1) + positions[...].astype(F32)).astype(BF)
    mask_own = dot(mask_in, choose).astype(BF)
    slot_own = dot(slot_in[...], choose).astype(BF)
    picked = (ids == iota((slots, rows), 1)).astype(F32)
    seen = jnp.sum(picked, axis=0, keepdims=True) > 0
    tile = (iota((tubs, rows), 0) == iota((tubs, rows), 1) % tubs).astype(F32).astype(BF)
    return jnp.where(seen, dot_tn(slot_own, picked.astype(BF)), dot_tn(mask_own, tile))


def split_pieces(values, count):
    out = []
    for _ in range(count):
        top = values.astype(BF).astype(F32)
        out.append(top)
        values = values - top
    return out


def attend_kernel(queries, column, out, kv_scr, msg_scr):
    blocks, tubs = queries.shape[0], 64
    nz = 2 * column.shape[0]
    vols = 4
    rows = vols * tubs
    slots = 64
    keys = nz * tubs
    for k in range(nz):
        side = k % 2
        pair = column[k // 2]
        block = pair[side * tubs : (side + 1) * tubs]
        ids_row = pair[2 * tubs :].astype(F32)[side : side + 1, :slots]
        picked = (ids_row == iota((rows, slots), 0).astype(F32)).astype(F32)
        seen = jnp.sum(picked, axis=1, keepdims=True) > 0
        placed = dot(picked.astype(BF), block[:, 64:])
        other = block[:, :64].astype(F32)
        other = jnp.concatenate([other] * vols, axis=0)
        mat = jnp.where(seen, placed, other).astype(BF)
        for v in range(vols):
            kv_scr[v, k * tubs : (k + 1) * tubs, :] = mat[v * tubs : (v + 1) * tubs]
    packed = queries[:, :tubs, :].reshape(blocks * tubs, 128)
    scale = math.log2(math.e) / math.sqrt(HDIM)

    def score(v):
        take = (iota((128, 64), 0) == iota((128, 64), 1) + HDIM * v) & (iota((128, 64), 1) < HDIM)
        query = dot(packed, take.astype(F32).astype(BF)).astype(BF)
        return dot_nt(kv_scr[v], query)

    def weigh(scores):
        top = jnp.max(scores, axis=0, keepdims=True)
        weights = jnp.exp2((scores - top) * scale)
        return top, jnp.sum(weights, axis=0, keepdims=True), weights.astype(BF)

    def put(v, top, total, weights):
        summed = dot_tn(kv_scr[v], weights)[HDIM:]
        stats = split_pieces(top * scale, 3) + split_pieces(total, 2)
        stats = jnp.concatenate(stats + [jnp.zeros((3, blocks * tubs), F32)], axis=0)
        half, side = v // 2, slice(64 * (v % 2), 64 * (v % 2) + 64)
        for b in range(blocks):
            cols = slice(b * tubs, (b + 1) * tubs)
            msg_scr[b, HDIM * half : HDIM * half + HDIM, side] = summed[:, cols]
            msg_scr[b, 64 + 8 * half : 72 + 8 * half, side] = stats[:, cols]

    scores, waiting = score(0), None
    for v in range(vols):
        later = score(v + 1) if v + 1 < vols else None
        weighed = weigh(scores)
        if waiting is not None:
            put(*waiting)
        waiting, scores = (v, *weighed), later
    put(*waiting)
    for b in range(blocks):
        out[b] = msg_scr[b].astype(BF)


def combine_kernel(message, w_attn_out, out):
    turn = plane_turn()
    parts = []
    for head in range(2):
        plane = jnp.where(turn == 0, head, 1 - head)
        sides = []
        for u in range(2):
            stats = [
                message[NY * plane + k, 64:, :].astype(F32)[8 * u : 8 * u + 8] for k in range(NY)
            ]
            tops = [s[0:1] + s[1:2] + s[2:3] for s in stats]
            best = functools.reduce(jnp.maximum, tops)
            fades = [jnp.exp2(t - best) for t in tops]
            total = sum(f * (s[3:4] + s[4:5]) for f, s in zip(fades, stats))
            value = sum(
                f * message[NY * plane + k, HDIM * u : HDIM * u + HDIM, :].astype(F32)
                for k, f in enumerate(fades)
            )
            sides.append(value / total)
        parts.append(jnp.concatenate(sides, axis=1))
    attended = jnp.concatenate(parts, axis=0).astype(BF)
    terms = dot_tn(w_attn_out[...], attended).astype(BF)
    count, feats, rows = out.shape
    for k in range(count):
        out[k] = terms[k * feats : (k + 1) * feats]


def finish_kernel(terms, lists, counts, mask_token, positions, slot_in, out):
    vols, tubs, feats = out.shape
    start = lax.axis_index("mp") * feats
    total = own_rows(start, lists, counts, mask_token, positions, slot_in, feats, vols * tubs)
    total = total + sum(terms[k].astype(F32) for k in range(terms.shape[0]))
    out[...] = total.T.astype(BF).reshape(vols, tubs, feats)


def call(kernel, out, *args, scratch=(), micros=0):
    many = isinstance(out, list)
    one = pl.BlockSpec(memory_space=pltpu.VMEM)
    cost = None
    if micros:
        cost = pl.CostEstimate(
            flops=micros * 10**9, bytes_accessed=micros * 10**6, transcendentals=0
        )
    return pl.pallas_call(
        kernel,
        out_shape=out,
        in_specs=[one] * len(args),
        out_specs=[one] * len(out) if many else one,
        scratch_shapes=list(scratch),
        compiler_params=pltpu.CompilerParams(vmem_limit_bytes=32 * 2**20),
        cost_estimate=cost,
    )(*args)


def shape(*dims, dtype=BF):
    return jax.ShapeDtypeStruct(dims, dtype)


def exchange(values, axis, groups=None):
    return lax.all_to_all(values, axis, 0, 0, axis_index_groups=groups, tiled=True)


def local(
    tokens,
    visible_lists,
    visible_counts,
    w_in,
    w_out,
    w_embed,
    mask_token,
    positions,
    w_qkv,
    w_attn_out,
):
    vols, tubs, part = tokens.shape
    rows = vols * tubs
    nmp = lax.axis_size("mp")
    ngroup, ncolumn = len(GROUP[0]), len(COLUMN[0])
    dec = w_embed.shape[1]
    feats = dec // nmp
    lists = visible_lists.reshape(1, -1)
    counts = visible_counts.reshape(1, -1)
    slots = lists.shape[1]
    w_rows = w_qkv.transpose(1, 2, 0)

    own = call(
        pick_kernel, shape(nmp, 80, 128), lists, tokens.reshape(rows, part), micros=10
    )
    full = exchange(own, "mp")
    terms = exchange(call(feed_kernel, shape(nmp, 80, 128), full, w_in, w_out), "mp")
    parts = call(embed_kernel, shape(len(ALONG_X[0]), slots, dec), terms, own, w_embed)
    parts = exchange(parts, "mp", ALONG_X)
    part_sum = call(join_kernel, shape(slots, dec, dtype=F32), parts)
    parts = lax.all_gather(part_sum, "mp", axis_index_groups=CORES)
    slot_in, group = call(
        project_kernel,
        [shape(slots, dec), shape(ngroup, 136, 128)],
        parts, lists, counts, mask_token, positions, w_rows,
    )
    group = exchange(group, "seq", GROUP)
    column = exchange(call(pair_kernel, shape(ncolumn, 136, 128), group), "seq", COLUMN)
    message = call(
        attend_kernel,
        shape(ngroup, 80, 128),
        group,
        column,
        scratch=[pltpu.VMEM((vols, 2 * ncolumn * tubs, 64), BF), pltpu.VMEM((ngroup, 80, 128), F32)],
    )
    message = exchange(message, "seq", GROUP)
    head_terms = call(combine_kernel, shape(nmp, feats, rows), message, w_attn_out)
    head_terms = exchange(head_terms, "mp")
    return call(
        finish_kernel,
        shape(vols, tubs, feats),
        head_terms, lists, counts, mask_token, positions, slot_in,
    )


def solution(mesh):
    in_specs = (
        P(None, "seq", "mp"),
        P("seq", None, None),
        P("seq", None),
        P(None, "mp"),
        P("mp", None),
        P("mp", None),
        P(),
        P("seq", None),
        P(None, None, "mp"),
        P("mp", None),
    )
    out_specs = P(None, "seq", "mp")
    return jax.shard_map(local, mesh=mesh, in_specs=in_specs, out_specs=out_specs, check_vma=False)
```

```python
import functools
import math

import jax
import jax.numpy as jnp
from jax import lax
from jax.experimental import pallas as pl
from jax.experimental.pallas import tpu as pltpu
from jax.sharding import PartitionSpec as P

HDIM = 32
NY = 4
NZ = 16
GROUP = [[(2 * k + p) * NY + y for y in range(NY) for p in range(2)] for k in range(NZ // 2)]
PAIR = [[(2 * k + p) * NY + y for p in range(2)] for k in range(NZ // 2) for y in range(NY)]
ALONG_Y = [[z * NY + y for y in range(NY)] for z in range(NZ)]
COLUMN = [
    [z * NY + y for z in range(NZ) if (z + z // (NZ // 2)) % 2 == head]
    for head in range(2)
    for y in range(NY)
]
ALONG_X = [[0, 2, 4, 6], [1, 3, 5, 7]]
CORES = [[0, 1], [2, 3], [4, 5], [6, 7]]
BF = jnp.bfloat16
F32 = jnp.float32
I32 = jnp.int32


def iota(shape, dim):
    return lax.broadcasted_iota(I32, shape, dim)


def dot(a, b):
    return jnp.dot(a, b, preferred_element_type=F32)


def dot_tn(a, b):
    return lax.dot_general(a, b, (((0,), (0,)), ((), ())), preferred_element_type=F32)


def dot_nt(a, b):
    return lax.dot_general(a, b, (((1,), (1,)), ((), ())), preferred_element_type=F32)


def norm_rows(values):
    mean_row = jnp.mean(values, axis=-1, keepdims=True)
    off = values - mean_row
    spread = jnp.mean(off * off, axis=-1, keepdims=True)
    return off * lax.rsqrt(spread + 1e-05)


def column_of(row):
    n = row.shape[1]
    return jnp.sum(jnp.where(iota((n, n), 0) == iota((n, n), 1), row, 0), axis=1, keepdims=True)


def plane_turn():
    return lax.axis_index("seq") // (NY * NZ // 2)


def live_row(lists, counts, rows):
    return jnp.where(counts > 0, lists, rows)


def fold_tail(block):
    tail = block[:, 128:]
    rows = tail.shape[0] // 4
    extra = jnp.concatenate([tail[k * rows : (k + 1) * rows] for k in range(4)], axis=1)
    return jnp.concatenate([block[:, :128], extra], axis=0)


def unfold_tail(folded):
    extra = folded[64:]
    tail = jnp.concatenate([extra[:, 32 * k : 32 * k + 32] for k in range(4)], axis=0)
    return jnp.concatenate([folded[:64], tail], axis=1)


def pick_kernel(lists, tokens, out):
    rows = tokens.shape[0]
    ids = column_of(lists[...])
    named = (ids == iota((ids.shape[0], rows), 1)).astype(F32).astype(BF)
    own = fold_tail(dot(named, tokens[...])).astype(BF)
    for k in range(out.shape[0]):
        out[k] = own


def feed_kernel(gathered, w_in, w_out, out):
    count = gathered.shape[0]
    part = w_in.shape[0] // count
    blocks = [unfold_tail(gathered[k].astype(F32)) for k in range(count)]
    width = count * part
    mean_row = sum(jnp.sum(b, axis=1, keepdims=True) for b in blocks) * (1.0 / width)
    blocks = [b - mean_row for b in blocks]
    spread = sum(jnp.sum(b * b, axis=1, keepdims=True) for b in blocks) * (1.0 / width)
    scale = lax.rsqrt(spread + 1e-05)
    hidden = None
    for k in range(count):
        term = dot((blocks[k] * scale).astype(BF), w_in[k * part : (k + 1) * part, :])
        hidden = term if hidden is None else hidden + term
    act = (0.5 * hidden * (1.0 + lax.erf(hidden * math.sqrt(0.5)))).astype(BF)
    terms = dot(act, w_out[...])
    for k in range(count):
        out[k] = fold_tail(terms[:, k * part : (k + 1) * part]).astype(BF)


def embed_kernel(terms, own, w_embed, out):
    total = own[0].astype(F32) + sum(terms[k].astype(F32) for k in range(terms.shape[0]))
    encoded = unfold_tail(total).astype(BF)
    value = dot(encoded, w_embed[...]).astype(BF)
    for k in range(out.shape[0]):
        out[k] = value


def join_kernel(parts, out):
    out[...] = sum(parts[k].astype(F32) for k in range(parts.shape[0]))


def project_kernel(parts, lists, counts, mask_token, positions, w_rows, slot_in, out):
    tubs = positions.shape[0]
    slots = lists.shape[1]
    ids_row = live_row(lists[...], counts[...], 4 * tubs)
    ids = column_of(ids_row)
    embedded = sum(parts[k] for k in range(parts.shape[0])).astype(BF).astype(F32)
    at = (ids % tubs == iota((slots, tubs), 1)).astype(F32).astype(BF)
    pos = positions[...]
    row_in = (embedded + dot(at, pos)).astype(BF)
    slot_in[...] = row_in
    mask_in = (mask_token[...].astype(F32).reshape(1, -1) + pos.astype(F32)).astype(BF)
    both = jnp.concatenate([mask_in, row_in], axis=0).astype(F32)
    w_q, w_k, w_v = w_rows[0], w_rows[1], w_rows[2]
    heads = [slice(0, HDIM), slice(HDIM, 2 * HDIM)]
    w_all = [w_q[h] for h in heads for _ in range(4)]
    w_all += [w[h] for h in heads for w in (w_k, w_v)]
    w_all = jnp.concatenate(w_all, axis=0)
    both = dot_nt(norm_rows(both).astype(BF), w_all).astype(BF)
    masked, proj = both[:tubs], both[tubs:]

    spot = (ids_row % tubs == iota((tubs, slots), 0)).astype(F32).astype(BF)
    of_volume = ids // tubs == iota((slots, 128), 1) // HDIM
    seen = dot(spot, of_volume.astype(F32).astype(BF)) > 0
    zero = jnp.zeros((slots, 128), BF)
    extra = jnp.concatenate([ids_row.astype(F32), jnp.zeros((1, 128 - slots), F32)], axis=1)
    extra = jnp.broadcast_to(extra, (8, 128)).astype(BF)
    turn = plane_turn()
    for head in range(2):
        cols = slice(128 * head, 128 * head + 128)
        placed = dot(spot, jnp.where(of_volume, proj[:, cols], zero))
        query = jnp.where(seen, placed, masked[:, cols].astype(F32)).astype(BF)
        cols = slice(256 + 64 * head, 256 + 64 * head + 64)
        block = jnp.concatenate([masked[:, cols], proj[:, cols]], axis=1)
        block = jnp.concatenate([query, block, extra], axis=0)
        out[jnp.where(turn == 0, head, 1 - head)] = block


def pair_kernel(pair, q_out, kv_out):
    first, second = pair[0], pair[1]
    q_out[...] = jnp.concatenate([first[:64], second[:64]], axis=0)
    odd = iota((8, 128), 0) % 2 == 1
    ids = jnp.where(odd, second[128:].astype(F32), first[128:].astype(F32)).astype(BF)
    block = jnp.concatenate([first[64:128], second[64:128], ids], axis=0)
    for k in range(kv_out.shape[0]):
        kv_out[k] = block


def own_rows(start, lists, counts, mask_token, positions, slot_in, feats, rows):
    tubs, dec = positions.shape
    slots = lists.shape[1]
    ids = column_of(live_row(lists[...], counts[...], rows))
    choose = (iota((dec, feats), 0) == iota((dec, feats), 1) + start).astype(F32).astype(BF)
    mask_in = (mask_token[...].astype(F32).reshape(1, -1) + positions[...].astype(F32)).astype(BF)
    mask_own = dot(mask_in, choose).astype(BF)
    slot_own = dot(slot_in[...], choose).astype(BF)
    picked = (ids == iota((slots, rows), 1)).astype(F32)
    seen = jnp.sum(picked, axis=0, keepdims=True) > 0
    tile = (iota((tubs, rows), 0) == iota((tubs, rows), 1) % tubs).astype(F32).astype(BF)
    return jnp.where(seen, dot_tn(slot_own, picked.astype(BF)), dot_tn(mask_own, tile))


def split_pieces(values, count):
    out = []
    for _ in range(count):
        top = values.astype(BF).astype(F32)
        out.append(top)
        values = values - top
    return out


def attend_kernel(queries, column, out, kv_scr, msg_scr):
    tubs = 64
    blocks = queries.shape[0] * queries.shape[1] // tubs
    nz = 2 * column.shape[0]
    vols = 4
    rows = vols * tubs
    slots = 64
    keys = nz * tubs
    for k in range(nz):
        side = k % 2
        pair = column[k // 2]
        block = pair[side * tubs : (side + 1) * tubs]
        ids_row = pair[2 * tubs :].astype(F32)[side : side + 1, :slots]
        picked = (ids_row == iota((rows, slots), 0).astype(F32)).astype(F32)
        seen = jnp.sum(picked, axis=1, keepdims=True) > 0
        placed = dot(picked.astype(BF), block[:, 64:])
        other = block[:, :64].astype(F32)
        other = jnp.concatenate([other] * vols, axis=0)
        mat = jnp.where(seen, placed, other).astype(BF)
        for v in range(vols):
            kv_scr[v, k * tubs : (k + 1) * tubs, :] = mat[v * tubs : (v + 1) * tubs]
    packed = queries[...].reshape(blocks * tubs, 128)
    scale = math.log2(math.e) / math.sqrt(HDIM)

    def score(v):
        take = (iota((128, 64), 0) == iota((128, 64), 1) + HDIM * v) & (iota((128, 64), 1) < HDIM)
        query = dot(packed, take.astype(F32).astype(BF)).astype(BF)
        return dot_nt(kv_scr[v], query)

    def weigh(scores):
        top = jnp.max(scores, axis=0, keepdims=True)
        weights = jnp.exp2((scores - top) * scale)
        return top, jnp.sum(weights, axis=0, keepdims=True), weights.astype(BF)

    def put(v, top, total, weights):
        summed = dot_tn(kv_scr[v], weights)[HDIM:]
        stats = split_pieces(top * scale, 3) + split_pieces(total, 2)
        stats = jnp.concatenate(stats + [jnp.zeros((3, blocks * tubs), F32)], axis=0)
        half, side = v // 2, slice(64 * (v % 2), 64 * (v % 2) + 64)
        for b in range(blocks):
            cols = slice(b * tubs, (b + 1) * tubs)
            msg_scr[b, HDIM * half : HDIM * half + HDIM, side] = summed[:, cols]
            msg_scr[b, 64 + 8 * half : 72 + 8 * half, side] = stats[:, cols]

    scores, waiting = score(0), None
    for v in range(vols):
        later = score(v + 1) if v + 1 < vols else None
        weighed = weigh(scores)
        if waiting is not None:
            put(*waiting)
        waiting, scores = (v, *weighed), later
    put(*waiting)
    for b in range(blocks):
        out[b] = msg_scr[b].astype(BF)


def combine_kernel(message, w_attn_out, out):
    turn = plane_turn()
    parts = []
    for head in range(2):
        plane = jnp.where(turn == 0, head, 1 - head)
        sides = []
        for u in range(2):
            stats = [
                message[2 * k + plane, 64:, :].astype(F32)[8 * u : 8 * u + 8] for k in range(NY)
            ]
            tops = [s[0:1] + s[1:2] + s[2:3] for s in stats]
            best = functools.reduce(jnp.maximum, tops)
            fades = [jnp.exp2(t - best) for t in tops]
            total = sum(f * (s[3:4] + s[4:5]) for f, s in zip(fades, stats))
            value = sum(
                f * message[2 * k + plane, HDIM * u : HDIM * u + HDIM, :].astype(F32)
                for k, f in enumerate(fades)
            )
            sides.append(value / total)
        parts.append(jnp.concatenate(sides, axis=1))
    attended = jnp.concatenate(parts, axis=0).astype(BF)
    terms = dot_tn(w_attn_out[...], attended).astype(BF)
    count, feats, rows = out.shape
    for k in range(count):
        out[k] = terms[k * feats : (k + 1) * feats]


def finish_kernel(terms, lists, counts, mask_token, positions, slot_in, out):
    vols, tubs, feats = out.shape
    start = lax.axis_index("mp") * feats
    total = own_rows(start, lists, counts, mask_token, positions, slot_in, feats, vols * tubs)
    total = total + sum(terms[k].astype(F32) for k in range(terms.shape[0]))
    out[...] = total.T.astype(BF).reshape(vols, tubs, feats)


def call(kernel, out, *args, scratch=(), micros=0):
    many = isinstance(out, list)
    one = pl.BlockSpec(memory_space=pltpu.VMEM)
    cost = None
    if micros:
        cost = pl.CostEstimate(
            flops=micros * 10**9, bytes_accessed=micros * 10**6, transcendentals=0
        )
    return pl.pallas_call(
        kernel,
        out_shape=out,
        in_specs=[one] * len(args),
        out_specs=[one] * len(out) if many else one,
        scratch_shapes=list(scratch),
        compiler_params=pltpu.CompilerParams(vmem_limit_bytes=32 * 2**20),
        cost_estimate=cost,
    )(*args)


def shape(*dims, dtype=BF):
    return jax.ShapeDtypeStruct(dims, dtype)


def exchange(values, axis, groups=None):
    return lax.all_to_all(values, axis, 0, 0, axis_index_groups=groups, tiled=True)


def local(
    tokens,
    visible_lists,
    visible_counts,
    w_in,
    w_out,
    w_embed,
    mask_token,
    positions,
    w_qkv,
    w_attn_out,
):
    vols, tubs, part = tokens.shape
    rows = vols * tubs
    nmp = lax.axis_size("mp")
    ngroup, ncolumn = len(GROUP[0]), len(COLUMN[0])
    dec = w_embed.shape[1]
    feats = dec // nmp
    lists = visible_lists.reshape(1, -1)
    counts = visible_counts.reshape(1, -1)
    slots = lists.shape[1]
    w_rows = w_qkv.transpose(1, 2, 0)

    own = call(
        pick_kernel, shape(nmp, 80, 128), lists, tokens.reshape(rows, part), micros=10
    )
    full = exchange(own, "mp")
    terms = exchange(call(feed_kernel, shape(nmp, 80, 128), full, w_in, w_out), "mp")
    parts = call(embed_kernel, shape(len(ALONG_X[0]), slots, dec), terms, own, w_embed)
    parts = exchange(parts, "mp", ALONG_X)
    part_sum = call(join_kernel, shape(slots, dec, dtype=F32), parts)
    parts = lax.all_gather(part_sum, "mp", axis_index_groups=CORES)
    slot_in, pair = call(
        project_kernel,
        [shape(slots, dec), shape(2, 136, 128)],
        parts, lists, counts, mask_token, positions, w_rows,
    )
    queries, column = call(
        pair_kernel,
        [shape(2 * tubs, 128), shape(ncolumn, 136, 128)],
        exchange(pair, "seq", PAIR),
    )
    column = exchange(column, "seq", COLUMN)
    queries = lax.all_gather(queries, "seq", axis_index_groups=ALONG_Y)
    message = call(
        attend_kernel,
        shape(ngroup, 80, 128),
        queries,
        column,
        scratch=[pltpu.VMEM((vols, 2 * ncolumn * tubs, 64), BF), pltpu.VMEM((ngroup, 80, 128), F32)],
    )
    message = exchange(message, "seq", GROUP)
    head_terms = call(combine_kernel, shape(nmp, feats, rows), message, w_attn_out)
    head_terms = exchange(head_terms, "mp")
    return call(
        finish_kernel,
        shape(vols, tubs, feats),
        head_terms, lists, counts, mask_token, positions, slot_in,
    )


def solution(mesh):
    in_specs = (
        P(None, "seq", "mp"),
        P("seq", None, None),
        P("seq", None),
        P(None, "mp"),
        P("mp", None),
        P("mp", None),
        P(),
        P("seq", None),
        P(None, None, "mp"),
        P("mp", None),
    )
    out_specs = P(None, "seq", "mp")
    return jax.shard_map(local, mesh=mesh, in_specs=in_specs, out_specs=out_specs, check_vma=False)
```

```python
import functools
import math

import jax
import jax.numpy as jnp
from jax import lax
from jax.experimental import pallas as pl
from jax.experimental.pallas import tpu as pltpu
from jax.sharding import PartitionSpec as P

HDIM = 32
NY = 4
NZ = 16
GROUP = [[(2 * k + p) * NY + y for y in range(NY) for p in range(2)] for k in range(NZ // 2)]
PAIR = [[(2 * k + p) * NY + y for p in range(2)] for k in range(NZ // 2) for y in range(NY)]
ALONG_Y = [[z * NY + y for y in range(NY)] for z in range(NZ)]
COLUMN = [
    [z * NY + y for z in range(NZ) if (z + z // (NZ // 2)) % 2 == head]
    for head in range(2)
    for y in range(NY)
]
ALONG_X = [[0, 2, 4, 6], [1, 3, 5, 7]]
CORES = [[0, 1], [2, 3], [4, 5], [6, 7]]
BF = jnp.bfloat16
F32 = jnp.float32
I32 = jnp.int32


def iota(shape, dim):
    return lax.broadcasted_iota(I32, shape, dim)


def dot(a, b):
    return jnp.dot(a, b, preferred_element_type=F32)


def dot_tn(a, b):
    return lax.dot_general(a, b, (((0,), (0,)), ((), ())), preferred_element_type=F32)


def dot_nt(a, b):
    return lax.dot_general(a, b, (((1,), (1,)), ((), ())), preferred_element_type=F32)


def norm_rows(values):
    mean_row = jnp.mean(values, axis=-1, keepdims=True)
    off = values - mean_row
    spread = jnp.mean(off * off, axis=-1, keepdims=True)
    return off * lax.rsqrt(spread + 1e-05)


def column_of(row):
    n = row.shape[1]
    return jnp.sum(jnp.where(iota((n, n), 0) == iota((n, n), 1), row, 0), axis=1, keepdims=True)


def plane_turn():
    return lax.axis_index("seq") // (NY * NZ // 2)


def live_row(lists, counts, rows):
    return jnp.where(counts > 0, lists, rows)


def fold_tail(block):
    tail = block[:, 128:]
    rows = tail.shape[0] // 4
    extra = jnp.concatenate([tail[k * rows : (k + 1) * rows] for k in range(4)], axis=1)
    return jnp.concatenate([block[:, :128], extra], axis=0)


def unfold_tail(folded):
    extra = folded[64:]
    tail = jnp.concatenate([extra[:, 32 * k : 32 * k + 32] for k in range(4)], axis=0)
    return jnp.concatenate([folded[:64], tail], axis=1)


def pick_kernel(lists, tokens, out):
    rows = tokens.shape[0]
    ids = column_of(lists[...])
    named = (ids == iota((ids.shape[0], rows), 1)).astype(F32).astype(BF)
    own = fold_tail(dot(named, tokens[...])).astype(BF)
    for k in range(out.shape[0]):
        out[k] = own


def feed_kernel(gathered, w_in, w_out, out):
    count = gathered.shape[0]
    part = w_in.shape[0] // count
    blocks = [unfold_tail(gathered[k].astype(F32)) for k in range(count)]
    width = count * part
    mean_row = sum(jnp.sum(b, axis=1, keepdims=True) for b in blocks) * (1.0 / width)
    blocks = [b - mean_row for b in blocks]
    spread = sum(jnp.sum(b * b, axis=1, keepdims=True) for b in blocks) * (1.0 / width)
    scale = lax.rsqrt(spread + 1e-05)
    hidden = None
    for k in range(count):
        term = dot((blocks[k] * scale).astype(BF), w_in[k * part : (k + 1) * part, :])
        hidden = term if hidden is None else hidden + term
    act = (0.5 * hidden * (1.0 + lax.erf(hidden * math.sqrt(0.5)))).astype(BF)
    terms = dot(act, w_out[...])
    for k in range(count):
        out[k] = fold_tail(terms[:, k * part : (k + 1) * part]).astype(BF)


def embed_kernel(terms, own, w_embed, out):
    total = own[0].astype(F32) + sum(terms[k].astype(F32) for k in range(terms.shape[0]))
    encoded = unfold_tail(total).astype(BF)
    value = dot(encoded, w_embed[...]).astype(BF)
    for k in range(out.shape[0]):
        out[k] = value


def join_kernel(parts, out):
    out[...] = sum(parts[k].astype(F32) for k in range(parts.shape[0]))


def project_kernel(parts, lists, counts, mask_token, positions, w_rows, slot_in, out):
    tubs = positions.shape[0]
    slots = lists.shape[1]
    ids_row = live_row(lists[...], counts[...], 4 * tubs)
    ids = column_of(ids_row)
    embedded = sum(parts[k] for k in range(parts.shape[0])).astype(BF).astype(F32)
    at = (ids % tubs == iota((slots, tubs), 1)).astype(F32).astype(BF)
    pos = positions[...]
    row_in = (embedded + dot(at, pos)).astype(BF)
    slot_in[...] = row_in
    mask_in = (mask_token[...].astype(F32).reshape(1, -1) + pos.astype(F32)).astype(BF)
    both = jnp.concatenate([mask_in, row_in], axis=0).astype(F32)
    w_q, w_k, w_v = w_rows[0], w_rows[1], w_rows[2]
    heads = [slice(0, HDIM), slice(HDIM, 2 * HDIM)]
    w_all = [w_q[h] for h in heads for _ in range(4)]
    w_all += [w[h] for h in heads for w in (w_k, w_v)]
    w_all = jnp.concatenate(w_all, axis=0)
    both = dot_nt(norm_rows(both).astype(BF), w_all).astype(BF)
    masked, proj = both[:tubs], both[tubs:]

    spot = (ids_row % tubs == iota((tubs, slots), 0)).astype(F32).astype(BF)
    of_volume = ids // tubs == iota((slots, 128), 1) // HDIM
    seen = dot(spot, of_volume.astype(F32).astype(BF)) > 0
    zero = jnp.zeros((slots, 128), BF)
    extra = jnp.concatenate([ids_row.astype(F32), jnp.zeros((1, 128 - slots), F32)], axis=1)
    extra = jnp.broadcast_to(extra, (8, 128)).astype(BF)
    for head in range(2):
        cols = slice(128 * head, 128 * head + 128)
        placed = dot(spot, jnp.where(of_volume, proj[:, cols], zero))
        query = jnp.where(seen, placed, masked[:, cols].astype(F32)).astype(BF)
        cols = slice(256 + 64 * head, 256 + 64 * head + 64)
        block = jnp.concatenate([masked[:, cols], proj[:, cols]], axis=1)
        block = jnp.concatenate([query, block, extra], axis=0)
        out[head] = block


def pair_kernel(pair, q_out, kv_out):
    head = (lax.axis_index("seq") // NY + plane_turn()) % 2
    first, second = pair[0, head], pair[1, head]
    q_out[...] = jnp.concatenate([first[:64], second[:64]], axis=0)
    odd = iota((8, 128), 0) % 2 == 1
    ids = jnp.where(odd, second[128:].astype(F32), first[128:].astype(F32)).astype(BF)
    block = jnp.concatenate([first[64:128], second[64:128], ids], axis=0)
    for k in range(kv_out.shape[0]):
        kv_out[k] = block


def own_kernel(lists, counts, mask_token, positions, slot_in, out):
    tubs, dec = positions.shape
    feats, rows = out.shape
    slots = lists.shape[1]
    start = lax.axis_index("mp") * feats
    ids = column_of(live_row(lists[...], counts[...], rows))
    choose = (iota((dec, feats), 0) == iota((dec, feats), 1) + start).astype(F32).astype(BF)
    mask_in = (mask_token[...].astype(F32).reshape(1, -1) + positions[...].astype(F32)).astype(BF)
    mask_own = dot(mask_in, choose).astype(BF)
    slot_own = dot(slot_in[...], choose).astype(BF)
    picked = (ids == iota((slots, rows), 1)).astype(F32)
    seen = jnp.sum(picked, axis=0, keepdims=True) > 0
    tile = (iota((tubs, rows), 0) == iota((tubs, rows), 1) % tubs).astype(F32).astype(BF)
    rows_own = jnp.where(seen, dot_tn(slot_own, picked.astype(BF)), dot_tn(mask_own, tile))
    out[...] = rows_own.astype(BF)


def split_pieces(values, count):
    out = []
    for _ in range(count):
        top = values.astype(BF).astype(F32)
        out.append(top)
        values = values - top
    return out


def attend_kernel(queries, column, out, kv_scr, ones_scr, msg_scr):
    tubs = 64
    blocks = queries.shape[0] * queries.shape[1] // tubs
    nz = 2 * column.shape[0]
    vols = 4
    rows = vols * tubs
    slots = 64
    keys = nz * tubs
    for k in range(nz):
        side = k % 2
        pair = column[k // 2]
        block = pair[side * tubs : (side + 1) * tubs]
        ids_row = pair[2 * tubs :].astype(F32)[side : side + 1, :slots]
        picked = (ids_row == iota((rows, slots), 0).astype(F32)).astype(F32)
        seen = jnp.sum(picked, axis=1, keepdims=True) > 0
        placed = dot(picked.astype(BF), block[:, 64:])
        other = block[:, :64].astype(F32)
        other = jnp.concatenate([other] * vols, axis=0)
        mat = jnp.where(seen, placed, other).astype(BF)
        ones = jnp.where(iota(mat.shape, 1) < HDIM, jnp.ones_like(mat), mat)
        for v in range(vols):
            kv_scr[v, k * tubs : (k + 1) * tubs, :] = mat[v * tubs : (v + 1) * tubs]
            ones_scr[v, k * tubs : (k + 1) * tubs, :] = ones[v * tubs : (v + 1) * tubs]
    packed = queries[...].reshape(blocks * tubs, 128)
    scale = math.log2(math.e) / math.sqrt(HDIM)

    def score(v):
        take = (iota((128, 64), 0) == iota((128, 64), 1) + HDIM * v) & (iota((128, 64), 1) < HDIM)
        query = dot(packed, take.astype(F32).astype(BF)).astype(BF)
        return dot_nt(kv_scr[v], query)

    def weigh(scores):
        top = jnp.max(scores, axis=0, keepdims=True)
        weights = jnp.exp2((scores - top) * scale)
        return top, weights.astype(BF)

    def put(v, top, weights):
        both = dot_tn(ones_scr[v], weights)
        total, summed = both[:1], both[HDIM:]
        stats = split_pieces(top * scale, 3) + split_pieces(total, 2)
        stats = jnp.concatenate(stats + [jnp.zeros((3, blocks * tubs), F32)], axis=0)
        half, side = v // 2, slice(64 * (v % 2), 64 * (v % 2) + 64)
        for b in range(blocks):
            cols = slice(b * tubs, (b + 1) * tubs)
            msg_scr[b, HDIM * half : HDIM * half + HDIM, side] = summed[:, cols]
            msg_scr[b, 64 + 8 * half : 72 + 8 * half, side] = stats[:, cols]

    scores, waiting = score(0), None
    for v in range(vols):
        later = score(v + 1) if v + 1 < vols else None
        weighed = weigh(scores)
        if waiting is not None:
            put(*waiting)
        waiting, scores = (v, *weighed), later
    put(*waiting)
    for b in range(blocks):
        out[b] = msg_scr[b].astype(BF)


def combine_kernel(message, w_attn_out, out):
    turn = plane_turn()
    parts = []
    for head in range(2):
        plane = jnp.where(turn == 0, head, 1 - head)
        sides = []
        for u in range(2):
            stats = [
                message[2 * k + plane, 64:, :].astype(F32)[8 * u : 8 * u + 8] for k in range(NY)
            ]
            tops = [s[0:1] + s[1:2] + s[2:3] for s in stats]
            best = functools.reduce(jnp.maximum, tops)
            fades = [jnp.exp2(t - best) for t in tops]
            total = sum(f * (s[3:4] + s[4:5]) for f, s in zip(fades, stats))
            value = sum(
                f * message[2 * k + plane, HDIM * u : HDIM * u + HDIM, :].astype(F32)
                for k, f in enumerate(fades)
            )
            sides.append(value / total)
        parts.append(jnp.concatenate(sides, axis=1))
    attended = jnp.concatenate(parts, axis=0).astype(BF)
    terms = dot_tn(w_attn_out[...], attended).astype(BF)
    count, feats, rows = out.shape
    for k in range(count):
        out[k] = terms[k * feats : (k + 1) * feats]


def finish_kernel(terms, dec_own, out):
    total = dec_own[...].astype(F32) + sum(terms[k].astype(F32) for k in range(terms.shape[0]))
    out[...] = total.T.astype(BF).reshape(out.shape)


def call(kernel, out, *args, scratch=(), micros=0):
    many = isinstance(out, list)
    one = pl.BlockSpec(memory_space=pltpu.VMEM)
    cost = None
    if micros:
        cost = pl.CostEstimate(
            flops=micros * 10**9, bytes_accessed=micros * 10**6, transcendentals=0
        )
    return pl.pallas_call(
        kernel,
        out_shape=out,
        in_specs=[one] * len(args),
        out_specs=[one] * len(out) if many else one,
        scratch_shapes=list(scratch),
        compiler_params=pltpu.CompilerParams(vmem_limit_bytes=32 * 2**20),
        cost_estimate=cost,
    )(*args)


def shape(*dims, dtype=BF):
    return jax.ShapeDtypeStruct(dims, dtype)


def exchange(values, axis, groups=None):
    return lax.all_to_all(values, axis, 0, 0, axis_index_groups=groups, tiled=True)


def local(
    tokens,
    visible_lists,
    visible_counts,
    w_in,
    w_out,
    w_embed,
    mask_token,
    positions,
    w_qkv,
    w_attn_out,
):
    vols, tubs, part = tokens.shape
    rows = vols * tubs
    nmp = lax.axis_size("mp")
    ngroup, ncolumn = len(GROUP[0]), len(COLUMN[0])
    dec = w_embed.shape[1]
    feats = dec // nmp
    lists = visible_lists.reshape(1, -1)
    counts = visible_counts.reshape(1, -1)
    slots = lists.shape[1]
    w_rows = w_qkv.transpose(1, 2, 0)

    own = call(
        pick_kernel, shape(nmp, 80, 128), lists, tokens.reshape(rows, part), micros=10
    )
    full = exchange(own, "mp")
    terms = exchange(call(feed_kernel, shape(nmp, 80, 128), full, w_in, w_out), "mp")
    parts = call(embed_kernel, shape(len(ALONG_X[0]), slots, dec), terms, own, w_embed)
    parts = exchange(parts, "mp", ALONG_X)
    part_sum = call(join_kernel, shape(slots, dec, dtype=F32), parts)
    parts = lax.all_gather(part_sum, "mp", axis_index_groups=CORES)
    slot_in, pair = call(
        project_kernel,
        [shape(slots, dec), shape(2, 136, 128)],
        parts, lists, counts, mask_token, positions, w_rows,
    )
    queries, column = call(
        pair_kernel,
        [shape(2 * tubs, 128), shape(ncolumn, 136, 128)],
        lax.all_gather(pair, "seq", axis_index_groups=PAIR),
    )
    column = exchange(column, "seq", COLUMN)
    queries = lax.all_gather(queries, "seq", axis_index_groups=ALONG_Y)
    dec_own = call(
        own_kernel, shape(feats, rows), lists, counts, mask_token, positions, slot_in
    )
    queries, dec_own = lax.optimization_barrier((queries, dec_own))
    message = call(
        attend_kernel,
        shape(ngroup, 80, 128),
        queries,
        column,
        scratch=[
            pltpu.VMEM((vols, 2 * ncolumn * tubs, 64), BF),
            pltpu.VMEM((vols, 2 * ncolumn * tubs, 64), BF),
            pltpu.VMEM((ngroup, 80, 128), F32),
        ],
    )
    message = exchange(message, "seq", GROUP)
    head_terms = call(combine_kernel, shape(nmp, feats, rows), message, w_attn_out)
    head_terms = exchange(head_terms, "mp")
    return call(finish_kernel, shape(vols, tubs, feats), head_terms, dec_own)


def solution(mesh):
    in_specs = (
        P(None, "seq", "mp"),
        P("seq", None, None),
        P("seq", None),
        P(None, "mp"),
        P("mp", None),
        P("mp", None),
        P(),
        P("seq", None),
        P(None, None, "mp"),
        P("mp", None),
    )
    out_specs = P(None, "seq", "mp")
    return jax.shard_map(local, mesh=mesh, in_specs=in_specs, out_specs=out_specs, check_vma=False)
```

```python
import functools
import math

import jax
import jax.numpy as jnp
from jax import lax
from jax.experimental import pallas as pl
from jax.experimental.pallas import tpu as pltpu
from jax.sharding import PartitionSpec as P

HDIM = 32
NY = 4
NZ = 16
GROUP = [[(2 * k + p) * NY + y for y in range(NY) for p in range(2)] for k in range(NZ // 2)]
PAIR = [[(2 * k + p) * NY + y for p in range(2)] for k in range(NZ // 2) for y in range(NY)]
ALONG_Y = [[z * NY + y for y in range(NY)] for z in range(NZ)]
SIDES = [[z for z in range(NZ) if bin(z).count("1") % 2 == side] for side in range(2)]
ORDER = (6, 1, 7, 0, 3, 4, 2, 5)
COLUMN = [[planes[k] * NY + y for k in ORDER] for planes in SIDES for y in range(NY)]
ALONG_X = [[0, 2, 4, 6], [1, 3, 5, 7]]
CORES = [[0, 1], [2, 3], [4, 5], [6, 7]]
BF = jnp.bfloat16
F32 = jnp.float32
I32 = jnp.int32


def iota(shape, dim):
    return lax.broadcasted_iota(I32, shape, dim)


def dot(a, b):
    return jnp.dot(a, b, preferred_element_type=F32)


def dot_tn(a, b):
    return lax.dot_general(a, b, (((0,), (0,)), ((), ())), preferred_element_type=F32)


def dot_nt(a, b):
    return lax.dot_general(a, b, (((1,), (1,)), ((), ())), preferred_element_type=F32)


def norm_rows(values):
    mean_row = jnp.mean(values, axis=-1, keepdims=True)
    off = values - mean_row
    spread = jnp.mean(off * off, axis=-1, keepdims=True)
    return off * lax.rsqrt(spread + 1e-05)


def column_of(row):
    n = row.shape[1]
    return jnp.sum(jnp.where(iota((n, n), 0) == iota((n, n), 1), row, 0), axis=1, keepdims=True)


def plane_turn():
    pair = lax.axis_index("seq") // (2 * NY)
    return (pair + pair // 2 + pair // 4) % 2


def live_row(lists, counts, rows):
    return jnp.where(counts > 0, lists, rows)


def fold_tail(block):
    tail = block[:, 128:]
    rows = tail.shape[0] // 4
    extra = jnp.concatenate([tail[k * rows : (k + 1) * rows] for k in range(4)], axis=1)
    return jnp.concatenate([block[:, :128], extra], axis=0)


def unfold_tail(folded):
    extra = folded[64:]
    tail = jnp.concatenate([extra[:, 32 * k : 32 * k + 32] for k in range(4)], axis=0)
    return jnp.concatenate([folded[:64], tail], axis=1)


def pick_kernel(lists, tokens, out):
    rows = tokens.shape[0]
    ids = column_of(lists[...])
    named = (ids == iota((ids.shape[0], rows), 1)).astype(F32).astype(BF)
    own = fold_tail(dot(named, tokens[...])).astype(BF)
    for k in range(out.shape[0]):
        out[k] = own


def feed_kernel(gathered, w_in, w_out, out):
    count = gathered.shape[0]
    part = w_in.shape[0] // count
    blocks = [unfold_tail(gathered[k].astype(F32)) for k in range(count)]
    width = count * part
    mean_row = sum(jnp.sum(b, axis=1, keepdims=True) for b in blocks) * (1.0 / width)
    blocks = [b - mean_row for b in blocks]
    spread = sum(jnp.sum(b * b, axis=1, keepdims=True) for b in blocks) * (1.0 / width)
    scale = lax.rsqrt(spread + 1e-05)
    hidden = None
    for k in range(count):
        term = dot((blocks[k] * scale).astype(BF), w_in[k * part : (k + 1) * part, :])
        hidden = term if hidden is None else hidden + term
    act = (0.5 * hidden * (1.0 + lax.erf(hidden * math.sqrt(0.5)))).astype(BF)
    terms = dot(act, w_out[...])
    for k in range(count):
        out[k] = fold_tail(terms[:, k * part : (k + 1) * part]).astype(BF)


def embed_kernel(terms, own, w_embed, out):
    total = own[0].astype(F32) + sum(terms[k].astype(F32) for k in range(terms.shape[0]))
    encoded = unfold_tail(total).astype(BF)
    value = dot(encoded, w_embed[...]).astype(BF)
    for k in range(out.shape[0]):
        out[k] = value


def join_kernel(parts, out):
    out[...] = sum(parts[k].astype(F32) for k in range(parts.shape[0]))


def project_kernel(parts, lists, counts, mask_token, positions, w_rows, slot_in, out):
    tubs = positions.shape[0]
    slots = lists.shape[1]
    ids_row = live_row(lists[...], counts[...], 4 * tubs)
    ids = column_of(ids_row)
    embedded = sum(parts[k] for k in range(parts.shape[0])).astype(BF).astype(F32)
    at = (ids % tubs == iota((slots, tubs), 1)).astype(F32).astype(BF)
    pos = positions[...]
    row_in = (embedded + dot(at, pos)).astype(BF)
    slot_in[...] = row_in
    mask_in = (mask_token[...].astype(F32).reshape(1, -1) + pos.astype(F32)).astype(BF)
    both = jnp.concatenate([mask_in, row_in], axis=0).astype(F32)
    w_q, w_k, w_v = w_rows[0], w_rows[1], w_rows[2]
    heads = [slice(0, HDIM), slice(HDIM, 2 * HDIM)]
    w_all = [w_q[h] for h in heads for _ in range(4)]
    w_all += [w[h] for h in heads for w in (w_k, w_v)]
    w_all = jnp.concatenate(w_all, axis=0)
    both = dot_nt(norm_rows(both).astype(BF), w_all).astype(BF)
    masked, proj = both[:tubs], both[tubs:]

    spot = (ids_row % tubs == iota((tubs, slots), 0)).astype(F32).astype(BF)
    of_volume = ids // tubs == iota((slots, 128), 1) // HDIM
    seen = dot(spot, of_volume.astype(F32).astype(BF)) > 0
    zero = jnp.zeros((slots, 128), BF)
    extra = jnp.concatenate([ids_row.astype(F32), jnp.zeros((1, 128 - slots), F32)], axis=1)
    extra = jnp.broadcast_to(extra, (8, 128)).astype(BF)
    for head in range(2):
        cols = slice(128 * head, 128 * head + 128)
        placed = dot(spot, jnp.where(of_volume, proj[:, cols], zero))
        query = jnp.where(seen, placed, masked[:, cols].astype(F32)).astype(BF)
        cols = slice(256 + 64 * head, 256 + 64 * head + 64)
        block = jnp.concatenate([masked[:, cols], proj[:, cols]], axis=1)
        block = jnp.concatenate([query, block, extra], axis=0)
        out[head] = block


def pair_kernel(pair, q_out, kv_out):
    head = (lax.axis_index("seq") // NY + plane_turn()) % 2
    first, second = pair[0, head], pair[1, head]
    q_out[...] = jnp.concatenate([first[:64], second[:64]], axis=0)
    odd = iota((8, 128), 0) % 2 == 1
    ids = jnp.where(odd, second[128:].astype(F32), first[128:].astype(F32)).astype(BF)
    block = jnp.concatenate([first[64:128], second[64:128], ids], axis=0)
    for k in range(kv_out.shape[0]):
        kv_out[k] = block


def own_kernel(lists, counts, mask_token, positions, slot_in, out):
    tubs, dec = positions.shape
    feats, rows = out.shape
    slots = lists.shape[1]
    start = lax.axis_index("mp") * feats
    ids = column_of(live_row(lists[...], counts[...], rows))
    choose = (iota((dec, feats), 0) == iota((dec, feats), 1) + start).astype(F32).astype(BF)
    mask_in = (mask_token[...].astype(F32).reshape(1, -1) + positions[...].astype(F32)).astype(BF)
    mask_own = dot(mask_in, choose).astype(BF)
    slot_own = dot(slot_in[...], choose).astype(BF)
    picked = (ids == iota((slots, rows), 1)).astype(F32)
    seen = jnp.sum(picked, axis=0, keepdims=True) > 0
    tile = (iota((tubs, rows), 0) == iota((tubs, rows), 1) % tubs).astype(F32).astype(BF)
    rows_own = jnp.where(seen, dot_tn(slot_own, picked.astype(BF)), dot_tn(mask_own, tile))
    out[...] = rows_own.astype(BF)


def split_pieces(values, count):
    out = []
    for _ in range(count):
        top = values.astype(BF).astype(F32)
        out.append(top)
        values = values - top
    return out


def attend_kernel(queries, column, out, kv_scr, ones_scr, msg_scr):
    tubs = 64
    blocks = queries.shape[0] * queries.shape[1] // tubs
    nz = 2 * column.shape[0]
    vols = 4
    rows = vols * tubs
    slots = 64
    keys = nz * tubs
    for k in range(nz):
        side = k % 2
        pair = column[k // 2]
        block = pair[side * tubs : (side + 1) * tubs]
        ids_row = pair[2 * tubs :].astype(F32)[side : side + 1, :slots]
        picked = (ids_row == iota((rows, slots), 0).astype(F32)).astype(F32)
        seen = jnp.sum(picked, axis=1, keepdims=True) > 0
        placed = dot(picked.astype(BF), block[:, 64:])
        other = block[:, :64].astype(F32)
        other = jnp.concatenate([other] * vols, axis=0)
        mat = jnp.where(seen, placed, other).astype(BF)
        ones = jnp.where(iota(mat.shape, 1) < HDIM, jnp.ones_like(mat), mat)
        for v in range(vols):
            kv_scr[v, k * tubs : (k + 1) * tubs, :] = mat[v * tubs : (v + 1) * tubs]
            ones_scr[v, k * tubs : (k + 1) * tubs, :] = ones[v * tubs : (v + 1) * tubs]
    packed = queries[...].reshape(blocks * tubs, 128)
    scale = math.log2(math.e) / math.sqrt(HDIM)

    def score(v):
        take = (iota((128, 64), 0) == iota((128, 64), 1) + HDIM * v) & (iota((128, 64), 1) < HDIM)
        query = dot(packed, take.astype(F32).astype(BF)).astype(BF)
        return dot_nt(kv_scr[v], query)

    def weigh(scores):
        top = jnp.max(scores, axis=0, keepdims=True)
        weights = jnp.exp2((scores - top) * scale)
        return top, weights.astype(BF)

    def put(v, top, weights):
        both = dot_tn(ones_scr[v], weights)
        total, summed = both[:1], both[HDIM:]
        stats = split_pieces(top * scale, 3) + split_pieces(total, 2)
        stats = jnp.concatenate(stats + [jnp.zeros((3, blocks * tubs), F32)], axis=0)
        half, side = v // 2, slice(64 * (v % 2), 64 * (v % 2) + 64)
        for b in range(blocks):
            cols = slice(b * tubs, (b + 1) * tubs)
            msg_scr[b, HDIM * half : HDIM * half + HDIM, side] = summed[:, cols]
            msg_scr[b, 64 + 8 * half : 72 + 8 * half, side] = stats[:, cols]

    scores, waiting = score(0), None
    for v in range(vols):
        later = score(v + 1) if v + 1 < vols else None
        weighed = weigh(scores)
        if waiting is not None:
            put(*waiting)
        waiting, scores = (v, *weighed), later
    put(*waiting)
    for b in range(blocks):
        out[b] = msg_scr[b].astype(BF)


def combine_kernel(message, w_attn_out, out):
    turn = plane_turn()
    parts = []
    for head in range(2):
        plane = jnp.where(turn == 0, head, 1 - head)
        sides = []
        for u in range(2):
            stats = [
                message[2 * k + plane, 64:, :].astype(F32)[8 * u : 8 * u + 8] for k in range(NY)
            ]
            tops = [s[0:1] + s[1:2] + s[2:3] for s in stats]
            best = functools.reduce(jnp.maximum, tops)
            fades = [jnp.exp2(t - best) for t in tops]
            total = sum(f * (s[3:4] + s[4:5]) for f, s in zip(fades, stats))
            value = sum(
                f * message[2 * k + plane, HDIM * u : HDIM * u + HDIM, :].astype(F32)
                for k, f in enumerate(fades)
            )
            sides.append(value / total)
        parts.append(jnp.concatenate(sides, axis=1))
    attended = jnp.concatenate(parts, axis=0).astype(BF)
    terms = dot_tn(w_attn_out[...], attended).astype(BF)
    count, feats, rows = out.shape
    for k in range(count):
        out[k] = terms[k * feats : (k + 1) * feats]


def finish_kernel(terms, dec_own, out):
    total = dec_own[...].astype(F32) + sum(terms[k].astype(F32) for k in range(terms.shape[0]))
    out[...] = total.T.astype(BF).reshape(out.shape)


def call(kernel, out, *args, scratch=(), micros=0):
    many = isinstance(out, list)
    one = pl.BlockSpec(memory_space=pltpu.VMEM)
    cost = None
    if micros:
        cost = pl.CostEstimate(
            flops=micros * 10**9, bytes_accessed=micros * 10**6, transcendentals=0
        )
    return pl.pallas_call(
        kernel,
        out_shape=out,
        in_specs=[one] * len(args),
        out_specs=[one] * len(out) if many else one,
        scratch_shapes=list(scratch),
        compiler_params=pltpu.CompilerParams(vmem_limit_bytes=32 * 2**20),
        cost_estimate=cost,
    )(*args)


def shape(*dims, dtype=BF):
    return jax.ShapeDtypeStruct(dims, dtype)


def exchange(values, axis, groups=None):
    return lax.all_to_all(values, axis, 0, 0, axis_index_groups=groups, tiled=True)


def local(
    tokens,
    visible_lists,
    visible_counts,
    w_in,
    w_out,
    w_embed,
    mask_token,
    positions,
    w_qkv,
    w_attn_out,
):
    vols, tubs, part = tokens.shape
    rows = vols * tubs
    nmp = lax.axis_size("mp")
    ngroup, ncolumn = len(GROUP[0]), len(COLUMN[0])
    dec = w_embed.shape[1]
    feats = dec // nmp
    lists = visible_lists.reshape(1, -1)
    counts = visible_counts.reshape(1, -1)
    slots = lists.shape[1]
    w_rows = w_qkv.transpose(1, 2, 0)

    own = call(
        pick_kernel, shape(nmp, 80, 128), lists, tokens.reshape(rows, part), micros=10
    )
    full = exchange(own, "mp")
    terms = exchange(call(feed_kernel, shape(nmp, 80, 128), full, w_in, w_out), "mp")
    parts = call(embed_kernel, shape(len(ALONG_X[0]), slots, dec), terms, own, w_embed)
    parts = exchange(parts, "mp", ALONG_X)
    part_sum = call(join_kernel, shape(slots, dec, dtype=F32), parts)
    parts = lax.all_gather(part_sum, "mp", axis_index_groups=CORES)
    slot_in, pair = call(
        project_kernel,
        [shape(slots, dec), shape(2, 136, 128)],
        parts, lists, counts, mask_token, positions, w_rows,
    )
    queries, column = call(
        pair_kernel,
        [shape(2 * tubs, 128), shape(ncolumn, 136, 128)],
        lax.all_gather(pair, "seq", axis_index_groups=PAIR),
    )
    column = exchange(column, "seq", COLUMN)
    queries = lax.all_gather(queries, "seq", axis_index_groups=ALONG_Y)
    dec_own = call(
        own_kernel, shape(feats, rows), lists, counts, mask_token, positions, slot_in
    )
    queries, dec_own = lax.optimization_barrier((queries, dec_own))
    message = call(
        attend_kernel,
        shape(ngroup, 80, 128),
        queries,
        column,
        scratch=[
            pltpu.VMEM((vols, 2 * ncolumn * tubs, 64), BF),
            pltpu.VMEM((vols, 2 * ncolumn * tubs, 64), BF),
            pltpu.VMEM((ngroup, 80, 128), F32),
        ],
    )
    message = exchange(message, "seq", GROUP)
    head_terms = call(combine_kernel, shape(nmp, feats, rows), message, w_attn_out)
    head_terms = exchange(head_terms, "mp")
    return call(finish_kernel, shape(vols, tubs, feats), head_terms, dec_own)


def solution(mesh):
    in_specs = (
        P(None, "seq", "mp"),
        P("seq", None, None),
        P("seq", None),
        P(None, "mp"),
        P("mp", None),
        P("mp", None),
        P(),
        P("seq", None),
        P(None, None, "mp"),
        P("mp", None),
    )
    out_specs = P(None, "seq", "mp")
    return jax.shard_map(local, mesh=mesh, in_specs=in_specs, out_specs=out_specs, check_vma=False)
```

```python
import functools
import math

import jax
import jax.numpy as jnp
from jax import lax
from jax.experimental import pallas as pl
from jax.experimental.pallas import tpu as pltpu
from jax.sharding import PartitionSpec as P

HDIM = 32
NY = 4
NZ = 16
GROUP = [[(2 * k + p) * NY + y for y in range(NY) for p in range(2)] for k in range(NZ // 2)]
PAIR = [[(2 * k + p) * NY + y for p in range(2)] for k in range(NZ // 2) for y in range(NY)]
ALONG_Y = [[z * NY + y for y in range(NY)] for z in range(NZ)]
SIDES = [[z for z in range(NZ) if bin(z).count("1") % 2 == side] for side in range(2)]
ORDER = (6, 2, 7, 0, 3, 4, 1, 5)
COLUMN = [[planes[k] * NY + y for k in ORDER] for planes in SIDES for y in range(NY)]
ALONG_X = [[0, 2, 4, 6], [1, 3, 5, 7]]
CORES = [[0, 1], [2, 3], [4, 5], [6, 7]]
BF = jnp.bfloat16
F32 = jnp.float32
I32 = jnp.int32


def iota(shape, dim):
    return lax.broadcasted_iota(I32, shape, dim)


def dot(a, b):
    return jnp.dot(a, b, preferred_element_type=F32)


def dot_tn(a, b):
    return lax.dot_general(a, b, (((0,), (0,)), ((), ())), preferred_element_type=F32)


def dot_nt(a, b):
    return lax.dot_general(a, b, (((1,), (1,)), ((), ())), preferred_element_type=F32)


def norm_rows(values):
    mean_row = jnp.mean(values, axis=-1, keepdims=True)
    off = values - mean_row
    spread = jnp.mean(off * off, axis=-1, keepdims=True)
    return off * lax.rsqrt(spread + 1e-05)


def column_of(row):
    n = row.shape[1]
    return jnp.sum(jnp.where(iota((n, n), 0) == iota((n, n), 1), row, 0), axis=1, keepdims=True)


def plane_turn():
    pair = lax.axis_index("seq") // (2 * NY)
    return (pair + pair // 2 + pair // 4) % 2


def live_row(lists, counts, rows):
    return jnp.where(counts > 0, lists, rows)


def fold_tail(block):
    tail = block[:, 128:]
    rows = tail.shape[0] // 4
    extra = jnp.concatenate([tail[k * rows : (k + 1) * rows] for k in range(4)], axis=1)
    return jnp.concatenate([block[:, :128], extra], axis=0)


def unfold_tail(folded):
    extra = folded[64:]
    tail = jnp.concatenate([extra[:, 32 * k : 32 * k + 32] for k in range(4)], axis=0)
    return jnp.concatenate([folded[:64], tail], axis=1)


def pick_kernel(lists, tokens, out):
    rows = tokens.shape[0]
    ids = column_of(lists[...])
    named = (ids == iota((ids.shape[0], rows), 1)).astype(F32).astype(BF)
    own = fold_tail(dot(named, tokens[...])).astype(BF)
    for k in range(out.shape[0]):
        out[k] = own


def feed_kernel(gathered, w_in, w_out, out):
    count = gathered.shape[0]
    part = w_in.shape[0] // count
    blocks = [unfold_tail(gathered[k].astype(F32)) for k in range(count)]
    width = count * part
    mean_row = sum(jnp.sum(b, axis=1, keepdims=True) for b in blocks) * (1.0 / width)
    blocks = [b - mean_row for b in blocks]
    spread = sum(jnp.sum(b * b, axis=1, keepdims=True) for b in blocks) * (1.0 / width)
    scale = lax.rsqrt(spread + 1e-05)
    hidden = None
    for k in range(count):
        term = dot((blocks[k] * scale).astype(BF), w_in[k * part : (k + 1) * part, :])
        hidden = term if hidden is None else hidden + term
    act = (0.5 * hidden * (1.0 + lax.erf(hidden * math.sqrt(0.5)))).astype(BF)
    terms = dot(act, w_out[...])
    for k in range(count):
        out[k] = fold_tail(terms[:, k * part : (k + 1) * part]).astype(BF)


def embed_kernel(terms, own, w_embed, out):
    total = own[0].astype(F32) + sum(terms[k].astype(F32) for k in range(terms.shape[0]))
    encoded = unfold_tail(total).astype(BF)
    value = dot(encoded, w_embed[...]).astype(BF)
    for k in range(out.shape[0]):
        out[k] = value


def join_kernel(parts, out):
    out[...] = sum(parts[k].astype(F32) for k in range(parts.shape[0]))


def project_kernel(parts, lists, counts, mask_token, positions, w_rows, slot_in, out):
    tubs = positions.shape[0]
    slots = lists.shape[1]
    ids_row = live_row(lists[...], counts[...], 4 * tubs)
    ids = column_of(ids_row)
    embedded = sum(parts[k] for k in range(parts.shape[0])).astype(BF).astype(F32)
    at = (ids % tubs == iota((slots, tubs), 1)).astype(F32).astype(BF)
    pos = positions[...]
    row_in = (embedded + dot(at, pos)).astype(BF)
    slot_in[...] = row_in
    mask_in = (mask_token[...].astype(F32).reshape(1, -1) + pos.astype(F32)).astype(BF)
    both = jnp.concatenate([mask_in, row_in], axis=0).astype(F32)
    w_q, w_k, w_v = w_rows[0], w_rows[1], w_rows[2]
    heads = [slice(0, HDIM), slice(HDIM, 2 * HDIM)]
    w_all = [w_q[h] for h in heads for _ in range(4)]
    w_all += [w[h] for h in heads for w in (w_k, w_v)]
    w_all = jnp.concatenate(w_all, axis=0)
    both = dot_nt(norm_rows(both).astype(BF), w_all).astype(BF)
    masked, proj = both[:tubs], both[tubs:]

    spot = (ids_row % tubs == iota((tubs, slots), 0)).astype(F32).astype(BF)
    of_volume = ids // tubs == iota((slots, 128), 1) // HDIM
    seen = dot(spot, of_volume.astype(F32).astype(BF)) > 0
    zero = jnp.zeros((slots, 128), BF)
    extra = jnp.concatenate([ids_row.astype(F32), jnp.zeros((1, 128 - slots), F32)], axis=1)
    extra = jnp.broadcast_to(extra, (8, 128)).astype(BF)
    for head in range(2):
        cols = slice(128 * head, 128 * head + 128)
        placed = dot(spot, jnp.where(of_volume, proj[:, cols], zero))
        query = jnp.where(seen, placed, masked[:, cols].astype(F32)).astype(BF)
        cols = slice(256 + 64 * head, 256 + 64 * head + 64)
        block = jnp.concatenate([masked[:, cols], proj[:, cols]], axis=1)
        block = jnp.concatenate([query, block, extra], axis=0)
        out[head] = block


def pair_kernel(pair, q_out, kv_out):
    head = (lax.axis_index("seq") // NY + plane_turn()) % 2
    first, second = pair[0, head], pair[1, head]
    q_out[...] = jnp.concatenate([first[:64], second[:64]], axis=0)
    odd = iota((8, 128), 0) % 2 == 1
    ids = jnp.where(odd, second[128:].astype(F32), first[128:].astype(F32)).astype(BF)
    block = jnp.concatenate([first[64:128], second[64:128], ids], axis=0)
    for k in range(kv_out.shape[0]):
        kv_out[k] = block


def own_kernel(lists, counts, mask_token, positions, slot_in, out):
    tubs, dec = positions.shape
    feats, rows = out.shape
    slots = lists.shape[1]
    start = lax.axis_index("mp") * feats
    ids = column_of(live_row(lists[...], counts[...], rows))
    choose = (iota((dec, feats), 0) == iota((dec, feats), 1) + start).astype(F32).astype(BF)
    mask_in = (mask_token[...].astype(F32).reshape(1, -1) + positions[...].astype(F32)).astype(BF)
    mask_own = dot(mask_in, choose).astype(BF)
    slot_own = dot(slot_in[...], choose).astype(BF)
    picked = (ids == iota((slots, rows), 1)).astype(F32)
    seen = jnp.sum(picked, axis=0, keepdims=True) > 0
    tile = (iota((tubs, rows), 0) == iota((tubs, rows), 1) % tubs).astype(F32).astype(BF)
    rows_own = jnp.where(seen, dot_tn(slot_own, picked.astype(BF)), dot_tn(mask_own, tile))
    out[...] = rows_own.astype(BF)


def split_pieces(values, count):
    out = []
    for _ in range(count):
        top = values.astype(BF).astype(F32)
        out.append(top)
        values = values - top
    return out


def attend_kernel(queries, column, out, kv_scr, ones_scr, msg_scr):
    tubs = 64
    blocks = queries.shape[0] * queries.shape[1] // tubs
    nz = 2 * column.shape[0]
    vols = 4
    rows = vols * tubs
    slots = 64
    keys = nz * tubs
    for k in range(nz):
        side = k % 2
        pair = column[k // 2]
        block = pair[side * tubs : (side + 1) * tubs]
        ids_row = pair[2 * tubs :].astype(F32)[side : side + 1, :slots]
        picked = (ids_row == iota((rows, slots), 0).astype(F32)).astype(F32)
        seen = jnp.sum(picked, axis=1, keepdims=True) > 0
        placed = dot(picked.astype(BF), block[:, 64:])
        other = block[:, :64].astype(F32)
        other = jnp.concatenate([other] * vols, axis=0)
        mat = jnp.where(seen, placed, other).astype(BF)
        ones = jnp.where(iota(mat.shape, 1) < HDIM, jnp.ones_like(mat), mat)
        for v in range(vols):
            kv_scr[v, k * tubs : (k + 1) * tubs, :] = mat[v * tubs : (v + 1) * tubs]
            ones_scr[v, k * tubs : (k + 1) * tubs, :] = ones[v * tubs : (v + 1) * tubs]
    packed = queries[...].reshape(blocks * tubs, 128)
    scale = math.log2(math.e) / math.sqrt(HDIM)

    def score(v):
        take = (iota((128, 64), 0) == iota((128, 64), 1) + HDIM * v) & (iota((128, 64), 1) < HDIM)
        query = dot(packed, take.astype(F32).astype(BF)).astype(BF)
        return dot_nt(kv_scr[v], query)

    def weigh(scores):
        top = jnp.max(scores, axis=0, keepdims=True)
        weights = jnp.exp2((scores - top) * scale)
        return top, weights.astype(BF)

    def put(v, top, weights):
        both = dot_tn(ones_scr[v], weights)
        total, summed = both[:1], both[HDIM:]
        stats = split_pieces(top * scale, 3) + split_pieces(total, 2)
        stats = jnp.concatenate(stats + [jnp.zeros((3, blocks * tubs), F32)], axis=0)
        half, side = v // 2, slice(64 * (v % 2), 64 * (v % 2) + 64)
        for b in range(blocks):
            cols = slice(b * tubs, (b + 1) * tubs)
            msg_scr[b, HDIM * half : HDIM * half + HDIM, side] = summed[:, cols]
            msg_scr[b, 64 + 8 * half : 72 + 8 * half, side] = stats[:, cols]

    scores, waiting = score(0), None
    for v in range(vols):
        later = score(v + 1) if v + 1 < vols else None
        weighed = weigh(scores)
        if waiting is not None:
            put(*waiting)
        waiting, scores = (v, *weighed), later
    put(*waiting)
    for b in range(blocks):
        out[b] = msg_scr[b].astype(BF)


def combine_kernel(message, w_attn_out, out):
    turn = plane_turn()
    parts = []
    for head in range(2):
        plane = jnp.where(turn == 0, head, 1 - head)
        sides = []
        for u in range(2):
            stats = [
                message[2 * k + plane, 64:, :].astype(F32)[8 * u : 8 * u + 8] for k in range(NY)
            ]
            tops = [s[0:1] + s[1:2] + s[2:3] for s in stats]
            best = functools.reduce(jnp.maximum, tops)
            fades = [jnp.exp2(t - best) for t in tops]
            total = sum(f * (s[3:4] + s[4:5]) for f, s in zip(fades, stats))
            value = sum(
                f * message[2 * k + plane, HDIM * u : HDIM * u + HDIM, :].astype(F32)
                for k, f in enumerate(fades)
            )
            sides.append(value / total)
        parts.append(jnp.concatenate(sides, axis=1))
    attended = jnp.concatenate(parts, axis=0).astype(BF)
    terms = dot_tn(w_attn_out[...], attended).astype(BF)
    count, feats, rows = out.shape
    for k in range(count):
        out[k] = terms[k * feats : (k + 1) * feats]


def finish_kernel(terms, dec_own, out):
    total = dec_own[...].astype(F32) + sum(terms[k].astype(F32) for k in range(terms.shape[0]))
    out[...] = total.T.astype(BF).reshape(out.shape)


def call(kernel, out, *args, scratch=(), micros=0):
    many = isinstance(out, list)
    one = pl.BlockSpec(memory_space=pltpu.VMEM)
    cost = None
    if micros:
        cost = pl.CostEstimate(
            flops=micros * 10**9, bytes_accessed=micros * 10**6, transcendentals=0
        )
    return pl.pallas_call(
        kernel,
        out_shape=out,
        in_specs=[one] * len(args),
        out_specs=[one] * len(out) if many else one,
        scratch_shapes=list(scratch),
        compiler_params=pltpu.CompilerParams(vmem_limit_bytes=32 * 2**20),
        cost_estimate=cost,
    )(*args)


def shape(*dims, dtype=BF):
    return jax.ShapeDtypeStruct(dims, dtype)


def exchange(values, axis, groups=None):
    return lax.all_to_all(values, axis, 0, 0, axis_index_groups=groups, tiled=True)


def local(
    tokens,
    visible_lists,
    visible_counts,
    w_in,
    w_out,
    w_embed,
    mask_token,
    positions,
    w_qkv,
    w_attn_out,
):
    vols, tubs, part = tokens.shape
    rows = vols * tubs
    nmp = lax.axis_size("mp")
    ngroup, ncolumn = len(GROUP[0]), len(COLUMN[0])
    dec = w_embed.shape[1]
    feats = dec // nmp
    lists = visible_lists.reshape(1, -1)
    counts = visible_counts.reshape(1, -1)
    slots = lists.shape[1]
    w_rows = w_qkv.transpose(1, 2, 0)

    own = call(
        pick_kernel, shape(nmp, 80, 128), lists, tokens.reshape(rows, part), micros=10
    )
    full = exchange(own, "mp")
    terms = exchange(call(feed_kernel, shape(nmp, 80, 128), full, w_in, w_out), "mp")
    parts = call(embed_kernel, shape(len(ALONG_X[0]), slots, dec), terms, own, w_embed)
    parts = exchange(parts, "mp", ALONG_X)
    part_sum = call(join_kernel, shape(slots, dec, dtype=F32), parts)
    parts = lax.all_gather(part_sum, "mp", axis_index_groups=CORES)
    slot_in, pair = call(
        project_kernel,
        [shape(slots, dec), shape(2, 136, 128)],
        parts, lists, counts, mask_token, positions, w_rows,
    )
    queries, column = call(
        pair_kernel,
        [shape(2 * tubs, 128), shape(ncolumn, 136, 128)],
        lax.all_gather(pair, "seq", axis_index_groups=PAIR),
    )
    column = exchange(column, "seq", COLUMN)
    queries = lax.all_gather(queries, "seq", axis_index_groups=ALONG_Y)
    dec_own = call(
        own_kernel, shape(feats, rows), lists, counts, mask_token, positions, slot_in
    )
    queries, dec_own = lax.optimization_barrier((queries, dec_own))
    message = call(
        attend_kernel,
        shape(ngroup, 80, 128),
        queries,
        column,
        scratch=[
            pltpu.VMEM((vols, 2 * ncolumn * tubs, 64), BF),
            pltpu.VMEM((vols, 2 * ncolumn * tubs, 64), BF),
            pltpu.VMEM((ngroup, 80, 128), F32),
        ],
    )
    message = exchange(message, "seq", GROUP)
    head_terms = call(combine_kernel, shape(nmp, feats, rows), message, w_attn_out)
    head_terms = exchange(head_terms, "mp")
    return call(finish_kernel, shape(vols, tubs, feats), head_terms, dec_own)


def solution(mesh):
    in_specs = (
        P(None, "seq", "mp"),
        P("seq", None, None),
        P("seq", None),
        P(None, "mp"),
        P("mp", None),
        P("mp", None),
        P(),
        P("seq", None),
        P(None, None, "mp"),
        P("mp", None),
    )
    out_specs = P(None, "seq", "mp")
    return jax.shard_map(local, mesh=mesh, in_specs=in_specs, out_specs=out_specs, check_vma=False)
```

```python
import functools
import math

import jax
import jax.numpy as jnp
from jax import lax
from jax.experimental import pallas as pl
from jax.experimental.pallas import tpu as pltpu
from jax.sharding import PartitionSpec as P

HDIM = 32
NY = 4
NZ = 16
GROUP = [[(2 * k + p) * NY + y for p in range(2) for y in range(NY)] for k in range(NZ // 2)]
PAIR = [[(2 * k + p) * NY + y for p in range(2)] for k in range(NZ // 2) for y in range(NY)]
ALONG_Y = [[z * NY + y for y in range(NY)] for z in range(NZ)]
SIDES = [[z for z in range(NZ) if bin(z).count("1") % 2 == side] for side in range(2)]
ORDER = (6, 2, 7, 0, 3, 4, 1, 5)
COLUMN = [[planes[k] * NY + y for k in ORDER] for planes in SIDES for y in range(NY)]
ALONG_X = [[0, 2, 4, 6], [1, 3, 5, 7]]
CORES = [[0, 1], [2, 3], [4, 5], [6, 7]]
BF = jnp.bfloat16
F32 = jnp.float32
I32 = jnp.int32


def iota(shape, dim):
    return lax.broadcasted_iota(I32, shape, dim)


def dot(a, b):
    return jnp.dot(a, b, preferred_element_type=F32)


def dot_tn(a, b):
    return lax.dot_general(a, b, (((0,), (0,)), ((), ())), preferred_element_type=F32)


def dot_nt(a, b):
    return lax.dot_general(a, b, (((1,), (1,)), ((), ())), preferred_element_type=F32)


def norm_rows(values):
    mean_row = jnp.mean(values, axis=-1, keepdims=True)
    off = values - mean_row
    spread = jnp.mean(off * off, axis=-1, keepdims=True)
    return off * lax.rsqrt(spread + 1e-05)


def column_of(row):
    n = row.shape[1]
    return jnp.sum(jnp.where(iota((n, n), 0) == iota((n, n), 1), row, 0), axis=1, keepdims=True)


def plane_turn():
    pair = lax.axis_index("seq") // (2 * NY)
    return (pair + pair // 2 + pair // 4) % 2


def live_row(lists, counts, rows):
    return jnp.where(counts > 0, lists, rows)


def fold_tail(block):
    tail = block[:, 128:]
    rows = tail.shape[0] // 4
    extra = jnp.concatenate([tail[k * rows : (k + 1) * rows] for k in range(4)], axis=1)
    return jnp.concatenate([block[:, :128], extra], axis=0)


def unfold_tail(folded):
    extra = folded[64:]
    tail = jnp.concatenate([extra[:, 32 * k : 32 * k + 32] for k in range(4)], axis=0)
    return jnp.concatenate([folded[:64], tail], axis=1)


def pick_kernel(lists, tokens, out):
    rows = tokens.shape[0]
    ids = column_of(lists[...])
    named = (ids == iota((ids.shape[0], rows), 1)).astype(F32).astype(BF)
    own = fold_tail(dot(named, tokens[...])).astype(BF)
    for k in range(out.shape[0]):
        out[k] = own


def feed_kernel(gathered, w_in, w_out, out):
    count = gathered.shape[0]
    part = w_in.shape[0] // count
    blocks = [unfold_tail(gathered[k].astype(F32)) for k in range(count)]
    width = count * part
    mean_row = sum(jnp.sum(b, axis=1, keepdims=True) for b in blocks) * (1.0 / width)
    blocks = [b - mean_row for b in blocks]
    spread = sum(jnp.sum(b * b, axis=1, keepdims=True) for b in blocks) * (1.0 / width)
    scale = lax.rsqrt(spread + 1e-05)
    hidden = None
    for k in range(count):
        term = dot((blocks[k] * scale).astype(BF), w_in[k * part : (k + 1) * part, :])
        hidden = term if hidden is None else hidden + term
    act = (0.5 * hidden * (1.0 + lax.erf(hidden * math.sqrt(0.5)))).astype(BF)
    terms = dot(act, w_out[...])
    for k in range(count):
        out[k] = fold_tail(terms[:, k * part : (k + 1) * part]).astype(BF)


def embed_kernel(terms, own, w_embed, out):
    total = own[0].astype(F32) + sum(terms[k].astype(F32) for k in range(terms.shape[0]))
    encoded = unfold_tail(total).astype(BF)
    value = dot(encoded, w_embed[...]).astype(BF)
    for k in range(out.shape[0]):
        out[k] = value


def join_kernel(parts, out):
    out[...] = sum(parts[k].astype(F32) for k in range(parts.shape[0]))


def project_kernel(parts, lists, counts, mask_token, positions, w_rows, slot_in, out):
    tubs = positions.shape[0]
    slots = lists.shape[1]
    ids_row = live_row(lists[...], counts[...], 4 * tubs)
    ids = column_of(ids_row)
    embedded = sum(parts[k] for k in range(parts.shape[0])).astype(BF).astype(F32)
    at = (ids % tubs == iota((slots, tubs), 1)).astype(F32).astype(BF)
    pos = positions[...]
    row_in = (embedded + dot(at, pos)).astype(BF)
    slot_in[...] = row_in
    mask_in = (mask_token[...].astype(F32).reshape(1, -1) + pos.astype(F32)).astype(BF)
    both = jnp.concatenate([mask_in, row_in], axis=0).astype(F32)
    w_q, w_k, w_v = w_rows[0], w_rows[1], w_rows[2]
    heads = [slice(0, HDIM), slice(HDIM, 2 * HDIM)]
    w_all = [w_q[h] for h in heads for _ in range(4)]
    w_all += [w[h] for h in heads for w in (w_k, w_v)]
    w_all = jnp.concatenate(w_all, axis=0)
    both = dot_nt(norm_rows(both).astype(BF), w_all).astype(BF)
    masked, proj = both[:tubs], both[tubs:]

    spot = (ids_row % tubs == iota((tubs, slots), 0)).astype(F32).astype(BF)
    of_volume = ids // tubs == iota((slots, 128), 1) // HDIM
    seen = dot(spot, of_volume.astype(F32).astype(BF)) > 0
    zero = jnp.zeros((slots, 128), BF)
    extra = jnp.concatenate([ids_row.astype(F32), jnp.zeros((1, 128 - slots), F32)], axis=1)
    extra = jnp.broadcast_to(extra, (8, 128)).astype(BF)
    for head in range(2):
        cols = slice(128 * head, 128 * head + 128)
        placed = dot(spot, jnp.where(of_volume, proj[:, cols], zero))
        query = jnp.where(seen, placed, masked[:, cols].astype(F32)).astype(BF)
        cols = slice(256 + 64 * head, 256 + 64 * head + 64)
        block = jnp.concatenate([masked[:, cols], proj[:, cols]], axis=1)
        block = jnp.concatenate([query, block, extra], axis=0)
        out[head] = block


def pair_kernel(pair, q_out, kv_out):
    head = (lax.axis_index("seq") // NY + plane_turn()) % 2
    first, second = pair[0, head], pair[1, head]
    q_out[...] = jnp.concatenate([first[:64], second[:64]], axis=0)
    odd = iota((8, 128), 0) % 2 == 1
    ids = jnp.where(odd, second[128:].astype(F32), first[128:].astype(F32)).astype(BF)
    block = jnp.concatenate([first[64:128], second[64:128], ids], axis=0)
    for k in range(kv_out.shape[0]):
        kv_out[k] = block


def own_kernel(lists, counts, mask_token, positions, slot_in, out):
    tubs, dec = positions.shape
    feats, rows = out.shape
    slots = lists.shape[1]
    start = lax.axis_index("mp") * feats
    ids = column_of(live_row(lists[...], counts[...], rows))
    choose = (iota((dec, feats), 0) == iota((dec, feats), 1) + start).astype(F32).astype(BF)
    mask_in = (mask_token[...].astype(F32).reshape(1, -1) + positions[...].astype(F32)).astype(BF)
    mask_own = dot(mask_in, choose).astype(BF)
    slot_own = dot(slot_in[...], choose).astype(BF)
    picked = (ids == iota((slots, rows), 1)).astype(F32)
    seen = jnp.sum(picked, axis=0, keepdims=True) > 0
    tile = (iota((tubs, rows), 0) == iota((tubs, rows), 1) % tubs).astype(F32).astype(BF)
    rows_own = jnp.where(seen, dot_tn(slot_own, picked.astype(BF)), dot_tn(mask_own, tile))
    out[...] = rows_own.astype(BF)


def split_pieces(values, count):
    out = []
    for _ in range(count):
        top = values.astype(BF).astype(F32)
        out.append(top)
        values = values - top
    return out


def attend_kernel(queries, column, out, kv_scr, ones_scr, msg_scr):
    tubs = 64
    blocks = queries.shape[0] * queries.shape[1] // tubs
    nz = 2 * column.shape[0]
    vols = 4
    rows = vols * tubs
    slots = 64
    keys = nz * tubs
    for k in range(nz):
        side = k % 2
        pair = column[k // 2]
        block = pair[side * tubs : (side + 1) * tubs]
        ids_row = pair[2 * tubs :].astype(F32)[side : side + 1, :slots]
        picked = (ids_row == iota((rows, slots), 0).astype(F32)).astype(F32)
        seen = jnp.sum(picked, axis=1, keepdims=True) > 0
        placed = dot(picked.astype(BF), block[:, 64:])
        other = block[:, :64].astype(F32)
        other = jnp.concatenate([other] * vols, axis=0)
        mat = jnp.where(seen, placed, other).astype(BF)
        ones = jnp.where(iota(mat.shape, 1) < HDIM, jnp.ones_like(mat), mat)
        for v in range(vols):
            kv_scr[v, k * tubs : (k + 1) * tubs, :] = mat[v * tubs : (v + 1) * tubs]
            ones_scr[v, k * tubs : (k + 1) * tubs, :] = ones[v * tubs : (v + 1) * tubs]
    packed = queries[...].reshape(blocks * tubs, 128)
    scale = math.log2(math.e) / math.sqrt(HDIM)

    def score(v):
        take = (iota((128, 64), 0) == iota((128, 64), 1) + HDIM * v) & (iota((128, 64), 1) < HDIM)
        query = dot(packed, take.astype(F32).astype(BF)).astype(BF)
        return dot_nt(kv_scr[v], query)

    def weigh(scores):
        top = jnp.max(scores, axis=0, keepdims=True)
        weights = jnp.exp2((scores - top) * scale)
        return top, weights.astype(BF)

    def put(v, top, weights):
        both = dot_tn(ones_scr[v], weights)
        total, summed = both[:1], both[HDIM:]
        stats = split_pieces(top * scale, 3) + split_pieces(total, 2)
        stats = jnp.concatenate(stats + [jnp.zeros((3, blocks * tubs), F32)], axis=0)
        half, side = v // 2, slice(64 * (v % 2), 64 * (v % 2) + 64)
        for b in range(blocks):
            cols = slice(b * tubs, (b + 1) * tubs)
            dest = b % 2 * NY + b // 2
            msg_scr[dest, HDIM * half : HDIM * half + HDIM, side] = summed[:, cols]
            msg_scr[dest, 64 + 8 * half : 72 + 8 * half, side] = stats[:, cols]

    scores, waiting = score(0), None
    for v in range(vols):
        later = score(v + 1) if v + 1 < vols else None
        weighed = weigh(scores)
        if waiting is not None:
            put(*waiting)
        waiting, scores = (v, *weighed), later
    put(*waiting)
    for b in range(blocks):
        out[b] = msg_scr[b].astype(BF)


def combine_kernel(message, w_attn_out, out):
    turn = plane_turn()
    parts = []
    for head in range(2):
        plane = jnp.where(turn == 0, head, 1 - head)
        sides = []
        for u in range(2):
            stats = [
                message[NY * plane + k, 64:, :].astype(F32)[8 * u : 8 * u + 8] for k in range(NY)
            ]
            tops = [s[0:1] + s[1:2] + s[2:3] for s in stats]
            best = functools.reduce(jnp.maximum, tops)
            fades = [jnp.exp2(t - best) for t in tops]
            total = sum(f * (s[3:4] + s[4:5]) for f, s in zip(fades, stats))
            value = sum(
                f * message[NY * plane + k, HDIM * u : HDIM * u + HDIM, :].astype(F32)
                for k, f in enumerate(fades)
            )
            sides.append(value / total)
        parts.append(jnp.concatenate(sides, axis=1))
    attended = jnp.concatenate(parts, axis=0).astype(BF)
    terms = dot_tn(w_attn_out[...], attended).astype(BF)
    count, feats, rows = out.shape
    for k in range(count):
        out[k] = terms[k * feats : (k + 1) * feats]


def finish_kernel(terms, dec_own, out):
    total = dec_own[...].astype(F32) + sum(terms[k].astype(F32) for k in range(terms.shape[0]))
    out[...] = total.T.astype(BF).reshape(out.shape)


def call(kernel, out, *args, scratch=(), micros=0):
    many = isinstance(out, list)
    one = pl.BlockSpec(memory_space=pltpu.VMEM)
    cost = None
    if micros:
        cost = pl.CostEstimate(
            flops=micros * 10**9, bytes_accessed=micros * 10**6, transcendentals=0
        )
    return pl.pallas_call(
        kernel,
        out_shape=out,
        in_specs=[one] * len(args),
        out_specs=[one] * len(out) if many else one,
        scratch_shapes=list(scratch),
        compiler_params=pltpu.CompilerParams(vmem_limit_bytes=32 * 2**20),
        cost_estimate=cost,
    )(*args)


def shape(*dims, dtype=BF):
    return jax.ShapeDtypeStruct(dims, dtype)


def exchange(values, axis, groups=None):
    return lax.all_to_all(values, axis, 0, 0, axis_index_groups=groups, tiled=True)


def local(
    tokens,
    visible_lists,
    visible_counts,
    w_in,
    w_out,
    w_embed,
    mask_token,
    positions,
    w_qkv,
    w_attn_out,
):
    vols, tubs, part = tokens.shape
    rows = vols * tubs
    nmp = lax.axis_size("mp")
    ngroup, ncolumn = len(GROUP[0]), len(COLUMN[0])
    dec = w_embed.shape[1]
    feats = dec // nmp
    lists = visible_lists.reshape(1, -1)
    counts = visible_counts.reshape(1, -1)
    slots = lists.shape[1]
    w_rows = w_qkv.transpose(1, 2, 0)

    own = call(
        pick_kernel, shape(nmp, 80, 128), lists, tokens.reshape(rows, part), micros=10
    )
    full = exchange(own, "mp")
    terms = exchange(call(feed_kernel, shape(nmp, 80, 128), full, w_in, w_out), "mp")
    parts = call(embed_kernel, shape(len(ALONG_X[0]), slots, dec), terms, own, w_embed)
    parts = exchange(parts, "mp", ALONG_X)
    part_sum = call(join_kernel, shape(slots, dec, dtype=F32), parts)
    parts = lax.all_gather(part_sum, "mp", axis_index_groups=CORES)
    slot_in, pair = call(
        project_kernel,
        [shape(slots, dec), shape(2, 136, 128)],
        parts, lists, counts, mask_token, positions, w_rows,
    )
    queries, column = call(
        pair_kernel,
        [shape(2 * tubs, 128), shape(ncolumn, 136, 128)],
        lax.all_gather(pair, "seq", axis_index_groups=PAIR),
    )
    column = exchange(column, "seq", COLUMN)
    queries = lax.all_gather(queries, "seq", axis_index_groups=ALONG_Y)
    dec_own = call(
        own_kernel, shape(feats, rows), lists, counts, mask_token, positions, slot_in
    )
    queries, dec_own = lax.optimization_barrier((queries, dec_own))
    message = call(
        attend_kernel,
        shape(ngroup, 80, 128),
        queries,
        column,
        scratch=[
            pltpu.VMEM((vols, 2 * ncolumn * tubs, 64), BF),
            pltpu.VMEM((vols, 2 * ncolumn * tubs, 64), BF),
            pltpu.VMEM((ngroup, 80, 128), F32),
        ],
    )
    message = exchange(message, "seq", GROUP)
    head_terms = call(combine_kernel, shape(nmp, feats, rows), message, w_attn_out)
    head_terms = exchange(head_terms, "mp")
    return call(finish_kernel, shape(vols, tubs, feats), head_terms, dec_own)


def solution(mesh):
    in_specs = (
        P(None, "seq", "mp"),
        P("seq", None, None),
        P("seq", None),
        P(None, "mp"),
        P("mp", None),
        P("mp", None),
        P(),
        P("seq", None),
        P(None, None, "mp"),
        P("mp", None),
    )
    out_specs = P(None, "seq", "mp")
    return jax.shard_map(local, mesh=mesh, in_specs=in_specs, out_specs=out_specs, check_vma=False)
```
